128 devices in a mesh: batch: 16 (over x_lo, z, core), depth: 4 (over y), height: 2 (over x_hi).
Axes of the slice: x: 4 (x_hi: 2, x_lo: 2; x = x_hi * 2 + x_lo), y: 4, z: 4, core: 2. Of those that a mesh axis runs over, the one named last changes fastest.
Arguments:
- inputs: bfloat16 [256, 16, 16, 8, 128], P('batch', 'depth', 'height'), may hold values from -6 to 6
- conv_early: bfloat16 [4, 4, 4, 64, 128], replicated, may hold values from -0.09375 to 0.09375
- conv_late: bfloat16 [3, 3, 3, 128, 128], replicated, may hold values from -0.109375 to 0.109375
- cotangent: bfloat16 [256, 8, 8, 8, 128], P(('batch', 'depth', 'height')), may hold values from -0.032958984 to 0.032958984
Outputs:
- activated: bfloat16 [256, 8, 8, 8, 128], P(('batch', 'depth', 'height'))
- grad_early: float32 [4, 4, 4, 64, 128], replicated
- grad_late: float32 [3, 3, 3, 128, 128], replicated
The draws below stay inside these ranges and needn't reach their ends.
All inputs are finite; a program needn't handle non-finite values.
Results may differ from the reference program's by a relative error of at most 0.0059.
Values may be sent and summed in bfloat16 or wider, within the bound.
No kernel may reach another device: no remote copies, remote signals or barrier semaphores. Data moves between devices by JAX's collectives and lax.ppermute only.
A program may use at most 128 MiB of HBM per device.

```python
import jax
import jax.numpy as jnp
from jax import lax

C0 = 64
C1 = 128
C2 = 128
V0 = 16
V1 = 8
SAMPLES = 256


def block_levels(stream_key, extent, pieces, least, largest):
    def one(dim, parts):
        heights = jax.random.uniform(jax.random.fold_in(jax.random.fold_in(stream_key, 6), dim), (parts,), jnp.float32, least / len(pieces), largest / len(pieces))
        return jnp.repeat(jnp.exp(heights), extent[dim] // parts).reshape((-1,) + (1,) * (len(extent) - dim - 1))

    gain = one(*pieces[0])
    for cut in pieces[1:]:
        gain = gain * one(*cut)
    return gain


def scatter_about(rng, extent, deviation, most, split=(), held_as=jnp.bfloat16):
    factor_of = block_levels(rng, extent, split, -0.22, 0.18) if split else 1.0
    array = jax.random.normal(rng, extent, jnp.float32) * deviation * factor_of
    return jnp.minimum(jnp.maximum(array, -most), most).astype(held_as)


def setup_inputs(seed: int = 0) -> dict:
    keys = jax.random.split(jax.random.key(seed), 5)
    return {
        "inputs": scatter_about(keys[0], (SAMPLES, V0, V0, V0 // 2, 2 * C0), 1.0, 6.0, ((0, 16), (1, 4), (2, 2))),
        "conv_early": scatter_about(keys[1], (4, 4, 4, C0, C1), (64 * C0) ** -0.5, 0.09375),
        "conv_late": scatter_about(keys[2], (3, 3, 3, C1, C2), (27 * C1) ** -0.5, 0.109375),
        "cotangent": scatter_about(keys[3], (SAMPLES, V1, V1, V1, C2), (2.0 / (SAMPLES * V1 ** 3) ** 0.5), 0.032958984, ((0, 128),)),
    }


def slope(value):
    sigma = jax.nn.sigmoid(value)
    return sigma * (1.0 + value * (1.0 - sigma))

def conv_cube(volume, kernel, stride, margin):
    result = lax.conv_general_dilated(volume[None], kernel, (stride, stride, stride), [(margin, margin)] * 3, dimension_numbers=('NDHWC', 'DHWIO', 'NDHWC'), precision=lax.Precision.HIGHEST)
    return result[0]

def reference(inputs, conv_early, conv_late, cotangent):
    early_kernel = conv_early.astype(jnp.float32)
    late_kernel = conv_late.astype(jnp.float32)

    def one_sample(carry, sample):
        volume_pairs, signal = sample
        volume = volume_pairs.astype(jnp.float32).reshape(V0, V0, V0, C0)
        early, pull_early = jax.vjp(lambda kernel: conv_cube(volume, kernel, 2, 1), early_kernel)
        hidden = lax.optimization_barrier(jax.nn.silu(early).astype(jnp.bfloat16))
        late, pull_late = jax.vjp(lambda field, kernel: conv_cube(field, kernel, 1, 1), hidden.astype(jnp.float32), late_kernel)
        activated = jax.nn.silu(late).astype(jnp.bfloat16)
        error_late = lax.optimization_barrier((signal.astype(jnp.float32) * slope(late)).astype(jnp.bfloat16))
        error_field, grad_late = pull_late(error_late.astype(jnp.float32))
        error_hidden = lax.optimization_barrier(error_field.astype(jnp.bfloat16))
        error_early = lax.optimization_barrier((error_hidden.astype(jnp.float32) * slope(early)).astype(jnp.bfloat16))
        grad_early, = pull_early(error_early.astype(jnp.float32))
        return ((carry[0] + grad_early, carry[1] + grad_late), activated)
    start = (jnp.zeros((4, 4, 4, C0, C1), jnp.float32), jnp.zeros((3, 3, 3, C1, C2), jnp.float32))
    sums, activated = lax.scan(one_sample, start, (inputs, cotangent))
    return (activated, sums[0], sums[1])
```

```python
import jax
import jax.numpy as jnp
from jax import lax
from jax.experimental import pallas as pl
from jax.experimental.pallas import tpu as pltpu
from jax.sharding import PartitionSpec as P

FINE = ("xl", "z", "core", "y", "xh")
BF16 = jnp.bfloat16
F32 = jnp.float32
SIDE = 8
LANES = 128
CELLS = SIDE * SIDE * 16
HALF = 4 * 4 * 4 * 64 // 2
HALF_LATE = 3 * 3 * 3 * 128 // 2
GRANULE = HALF_LATE // 9
SHARE = HALF // 64
RING = 4


def shifted(rows, by, lane=None):
    moved = pltpu.roll(rows, by % SIDE, 1)
    width = lax.broadcasted_iota(jnp.int32, rows.shape, 1)
    return jnp.where(width == (0 if by == 1 else SIDE - 1), 0.0, moved)


def three_widths(rows):
    return jnp.concatenate([shifted(rows, 1), rows, shifted(rows, -1)], axis=-1)


def clear_rim(ref, size):
    lanes = ref.shape[-1]
    slab = jnp.zeros((size, 16, lanes), BF16)
    ref[0] = slab
    ref[size - 1] = slab
    ref[:, 0] = slab
    ref[:, size - 1] = slab


def cube_conv(field, blocks, total):
    def product(first, count, weights, transposed):
        rows = jnp.concatenate([field[first : first + count, kh : kh + SIDE] for kh in range(3)], axis=-1)
        dims = (((1,), (1 if transposed else 0,)), ((), ()))
        return lax.dot_general(
            rows.reshape(count * LANES, 9 * LANES), weights, dims, preferred_element_type=F32
        )

    (first, transposed), (second, _), (third, _) = (blocks(kd) for kd in range(3))
    two = product(0, 9, jnp.concatenate([first, second], axis=0 if transposed else 1), transposed)
    total[...] = two[0:CELLS, 0:LANES] + two[LANES : LANES + CELLS, LANES:]
    total[...] += product(2, SIDE, third, transposed)


def early_kernel(received, conv_early, hidden, volume, slope_early, total):
    depth_blocks, height_blocks = 4, 2
    blank = jnp.zeros((9, 16, 2 * LANES), BF16)
    for dp in range(2):
        for hp in range(2):
            volume[2 * dp + hp, 0 if dp else 8] = blank
            volume[2 * dp + hp, :, 0 if hp else 8] = blank

    for block in range(depth_blocks * height_blocks):
        db, hb = divmod(block, height_blocks)
        for layer in range(4):
            half, dp = layer // 2, layer % 2
            samples = [
                received[block, s, layer].astype(F32).reshape(4, 2, SIDE, LANES) for s in range(2)
            ]
            for hp in range(2):
                centre = jnp.stack([x[:, hp] for x in samples], axis=1).reshape(8, SIDE, LANES)
                lane = lax.broadcasted_iota(jnp.int32, centre.shape, 2)
                sides = jnp.where(lane < LANES // 2, shifted(centre, -1), shifted(centre, 1))
                both = jnp.concatenate([centre, sides], axis=-1).reshape(4, 16, 2 * LANES)
                volume[2 * dp + hp, 2 * db + half + dp, 4 * hb + hp : 4 * hb + hp + 4] = both.astype(
                    BF16
                )

    def early_taps(kd, kh):
        tap = 4 * kd + kh
        return jnp.concatenate([conv_early[tap, 64:256], conv_early[tap, 0:64]], axis=0)

    for dp in range(2):
        rows = jnp.concatenate(
            [volume[2 * dp + (kh + 1) % 2, :, kh // 2 : kh // 2 + SIDE] for kh in range(4)], axis=-1
        )
        weights = [
            jnp.concatenate([early_taps(kd, kh) for kh in range(4)], axis=0) for kd in (1 - dp, 3 - dp)
        ]
        two = jnp.dot(
            rows.reshape(9 * LANES, 8 * LANES),
            jnp.concatenate(weights, axis=1),
            preferred_element_type=F32,
        )
        both = two[0:CELLS, 0:LANES] + two[LANES : LANES + CELLS, LANES:]
        if dp:
            total[...] += both
        else:
            total[...] = both

    clear_rim(hidden, 10)
    for d in range(SIDE):
        rows = pl.ds(d * LANES, LANES)
        early = total[rows]
        sigma = jax.nn.sigmoid(early)
        slope_early[rows] = sigma * (1.0 + early * (1.0 - sigma))
        value = (early * sigma).reshape(16, SIDE, LANES)
        hidden[d + 1, 1:9] = three_widths(value).reshape(SIDE, 16, 3 * LANES).astype(BF16)


def late_kernel(
    core, hidden, conv_late, cotangent, activated, kept, sent, error, hidden_t, total, grads
):
    def late_block(kd):
        return conv_late[3 * kd : 3 * kd + 3].reshape(9 * LANES, LANES), False

    cube_conv(hidden, late_block, total)

    clear_rim(error, 10)
    for d in range(SIDE):
        rows = pl.ds(d * LANES, LANES)
        late = total[rows]
        sigma = jax.nn.sigmoid(late)
        out = (late * sigma).reshape(SIDE, 2, SIDE, LANES)
        for s in range(2):
            activated[s, d] = out[:, s].reshape(SIDE * SIDE, LANES).astype(BF16)
        value = (cotangent[rows].astype(F32) * (sigma * (1.0 + late * (1.0 - sigma)))).reshape(16, SIDE, LANES)
        error[d + 1, 1:9] = three_widths(value).reshape(SIDE, 16, 3 * LANES).astype(BF16)

    grads[:, HALF_LATE:] = jnp.zeros((2, HALF - HALF_LATE, LANES), BF16)
    for d in range(SIDE):
        hidden_t[:, d * LANES : (d + 1) * LANES] = hidden[d + 1, 1:9].reshape(LANES, 3 * LANES).T

    for kh in range(3):
        for depth_taps in ((0, 1), (2,)):
            moved = [
                error[2 - kd : 10 - kd, 2 - kh : 10 - kh, :, LANES : 2 * LANES].reshape(CELLS, LANES)
                for kd in depth_taps
            ]
            side = moved[0] if len(moved) == 1 else jnp.concatenate(moved, axis=1)
            grad = jnp.dot(hidden_t[...], side, preferred_element_type=F32).astype(BF16)
            for column, kd in enumerate(depth_taps):
                for part in range(2):
                    half, granule = divmod(2 * (3 * kd + kh) + part, 9)
                    grads[
                        jnp.where(core[0] == half, 0, 1), granule * GRANULE : (granule + 1) * GRANULE
                    ] = grad[part * GRANULE : (part + 1) * GRANULE, column * LANES : (column + 1) * LANES]
    kept[...] = grads[0]
    sent[...] = grads[1]


def backward_kernel(
    core, conv_late, volume, error, slope_early, kept, sent, volume_t, error_early, total, grads
):
    clear_rim(error_early, 10)

    def back_block(kd):
        taps = [
            conv_late[3 * (2 - kd) + 2 - kh, (2 - kw) * LANES : (3 - kw) * LANES]
            for kh in range(3)
            for kw in range(3)
        ]
        return jnp.concatenate(taps, axis=1), True

    cube_conv(error, back_block, total)

    for d in range(SIDE):
        rows = pl.ds(d * LANES, LANES)
        value = total[rows].astype(BF16).astype(F32) * slope_early[rows]
        error_early[d + 1, 1:9] = value.astype(BF16).reshape(SIDE, 16, LANES)

    for phase in range(4):
        dp, hp = phase // 2, phase % 2
        for d in range(SIDE):
            volume_t[phase, :, d * LANES : (d + 1) * LANES] = (
                volume[phase, d + dp, hp : hp + SIDE].reshape(LANES, 2 * LANES).T
            )
    for phase in range(4):
        dp, hp = phase // 2, phase % 2
        for first in range(2):
            depth = dp + 1 - first
            moved = [
                error_early[depth : depth + SIDE, hp + 1 - second : hp + 1 - second + SIDE].reshape(
                    CELLS, LANES
                )
                for second in range(2)
            ]
            grad = jnp.dot(
                volume_t[phase], jnp.concatenate(moved, axis=1), preferred_element_type=F32
            ).astype(BF16)
            keep = jnp.where(core[0] == first, 0, 1)
            for second in range(2):
                tap = 4 * (2 * first + 1 - dp) + 2 * second + 1 - hp
                lanes = slice(second * LANES, (second + 1) * LANES)
                at = (tap - 8 * first) * 2 * LANES
                grads[keep, at + 64 : at + 256] = grad[0:192, lanes]
                grads[keep, at : at + 64] = grad[192:256, lanes]
    kept[...] = grads[0]
    sent[...] = grads[1]


VMEM = pl.BlockSpec(memory_space=pltpu.VMEM)
SMEM = pl.BlockSpec(memory_space=pltpu.SMEM)
ANY = pl.BlockSpec(memory_space=pl.ANY)
SMALL = pltpu.CompilerParams(vmem_limit_bytes=12 * 1024 * 1024)
LIMIT = pltpu.CompilerParams(vmem_limit_bytes=24 * 1024 * 1024)
VOLUME = (4, 9, 9, 16, 2 * LANES)
FIELD = (10, 10, 16, 3 * LANES)


HALF_ROWS = jax.ShapeDtypeStruct((HALF, LANES), BF16)


def cost(products, transcendentals=0):
    return pl.CostEstimate(
        flops=2 * CELLS * LANES * products,
        bytes_accessed=8 * 1024 * 1024,
        transcendentals=transcendentals,
    )


def early_layer(received, conv_early):
    return pl.pallas_call(
        early_kernel,
        out_shape=(
            jax.ShapeDtypeStruct(FIELD, BF16),
            jax.ShapeDtypeStruct(VOLUME, BF16),
            jax.ShapeDtypeStruct((CELLS, LANES), F32),
        ),
        in_specs=[VMEM, VMEM],
        out_specs=(VMEM,) * 3,
        scratch_shapes=[pltpu.VMEM((CELLS, LANES), F32)],
        compiler_params=LIMIT,
        cost_estimate=cost(16 * 256, CELLS * LANES),
    )(received, conv_early)


def late_layer(core, hidden, conv_late, cotangent):
    return pl.pallas_call(
        late_kernel,
        out_shape=(
            jax.ShapeDtypeStruct((2, SIDE, SIDE * SIDE, LANES), BF16),
            HALF_ROWS,
            HALF_ROWS,
            jax.ShapeDtypeStruct(FIELD, BF16),
        ),
        in_specs=[SMEM, VMEM, VMEM, VMEM],
        out_specs=(VMEM,) * 4,
        scratch_shapes=[
            pltpu.VMEM((3 * LANES, CELLS), BF16),
            pltpu.VMEM((CELLS, LANES), F32),
            pltpu.VMEM((2, HALF, LANES), BF16),
        ],
        compiler_params=LIMIT,
        cost_estimate=cost(2 * 27 * LANES, CELLS * LANES),
    )(core, hidden, conv_late, cotangent)


def backward(core, conv_late, volume, error, slope_early):
    return pl.pallas_call(
        backward_kernel,
        out_shape=(HALF_ROWS, HALF_ROWS),
        in_specs=[SMEM, VMEM, VMEM, VMEM, VMEM],
        out_specs=(VMEM, VMEM),
        scratch_shapes=[
            pltpu.VMEM((4, 2 * LANES, CELLS), BF16),
            pltpu.VMEM((10, 10, 16, LANES), BF16),
            pltpu.VMEM((CELLS, LANES), F32),
            pltpu.VMEM((2, HALF, LANES), BF16),
        ],
        compiler_params=LIMIT,
        cost_estimate=cost(16 * 256 + 27 * LANES),
    )(core, conv_late, volume, error, slope_early)


def ring_place(core):
    return jnp.where(core == 0, lax.axis_index("z"), lax.axis_index("y"))


def chip_routes():
    shifts = [[], [], [], []]
    planes = {}
    for xl in range(2):
        for z in range(RING):
            for core in range(2):
                for y in range(RING):
                    for xh in range(2):
                        index = lambda z, y: (((xl * RING + z) * 2 + core) * RING + y) * 2 + xh
                        for by, pairs in enumerate(shifts):
                            to = ((z + by) % RING, y) if core == 0 else (z, (y + by) % RING)
                            pairs.append((index(z, y), index(*to)))
                        planes.setdefault((core, z if core == 0 else y), []).append(index(z, y))
    return shifts, [planes[key] for key in sorted(planes)]


def pair_kernel(place, early, early_other, late, late_other, *blocks):
    rows = HALF // RING
    for n, block in enumerate(blocks):
        start = ((place[0] + n) % RING) * rows
        for kept, other, first in ((early, early_other, 0), (late, late_other, SHARE)):
            part = pl.ds(pl.multiple_of(start, rows), rows)
            value = (kept[part].astype(F32) + other[part].astype(F32)).astype(BF16)
            block[:, first : first + SHARE] = value.reshape(16, SHARE, LANES)


def pair_sums(place, early, early_other, late, late_other):
    block = jax.ShapeDtypeStruct((16, 2 * SHARE, LANES), BF16)
    return pl.pallas_call(
        pair_kernel,
        out_shape=(block,) * RING,
        in_specs=[SMEM] + [VMEM] * 4,
        out_specs=(VMEM,) * RING,
        compiler_params=SMALL,
        cost_estimate=pl.CostEstimate(flops=0, bytes_accessed=4 * 1024 * 1024, transcendentals=0),
    )(place.reshape(1), early, early_other, late, late_other)


def swapped(block):
    return lax.ppermute(block, "core", [(0, 1), (1, 0)])


def summed(core, early, early_other, late, late_other):
    shifts, planes = chip_routes()
    exchange = lambda blocks, groups: lax.all_to_all(
        blocks, FINE, split_axis=0, concat_axis=0, axis_index_groups=groups, tiled=True
    )
    blocks = pair_sums(ring_place(core), early, early_other, late, late_other)
    total = blocks[0].astype(F32)
    for by in range(1, RING):
        total += lax.ppermute(blocks[by], FINE, shifts[by]).astype(F32)
    shares = exchange(total.astype(BF16), planes)
    share = jnp.sum(shares.astype(F32), axis=0).astype(BF16)
    wholes = [sum(planes[core * RING : (core + 1) * RING], []) for core in range(2)]
    return exchange(jnp.broadcast_to(share[None], (64,) + share.shape), wholes)


def place_kernel(half, shares, *refs):
    early, late, wide_early, wide_late, sems = refs[-5:]
    copies = []
    for chunk in range(4):
        for n in range(16 * chunk, 16 * (chunk + 1)):
            at = n * SHARE
            wide_early[at : at + SHARE] = shares[n, :SHARE].astype(F32)
            if at < HALF_LATE:
                wide_late[at : at + SHARE] = shares[n, SHARE:].astype(F32)
        low, high = 16 * chunk * SHARE, 16 * (chunk + 1) * SHARE
        for wide, out, rows, sem in ((wide_early, early, HALF, 0), (wide_late, late, HALF_LATE, 4)):
            size = min(high, rows) - low
            start = pl.multiple_of(half[0] * rows + low, 8)
            copy = pltpu.make_async_copy(
                wide.at[pl.ds(low, size)], out.at[pl.ds(start, size)], sems.at[sem + chunk]
            )
            copy.start()
            copies.append(copy)
    for copy in copies:
        copy.wait()


def placed(half, shares, so_far=()):
    return pl.pallas_call(
        place_kernel,
        out_shape=(
            jax.ShapeDtypeStruct((2 * HALF, LANES), F32),
            jax.ShapeDtypeStruct((2 * HALF_LATE, LANES), F32),
        ),
        in_specs=[SMEM, VMEM] + [ANY] * len(so_far),
        out_specs=(ANY, ANY),
        input_output_aliases={2 + n: n for n in range(len(so_far))},
        scratch_shapes=[
            pltpu.VMEM((HALF, LANES), F32),
            pltpu.VMEM((HALF_LATE, LANES), F32),
            pltpu.SemaphoreType.DMA((8,)),
        ],
        compiler_params=SMALL,
        cost_estimate=pl.CostEstimate(flops=0, bytes_accessed=3 * 1024 * 1024, transcendentals=0),
    )(half.reshape(1), shares, *so_far)


def per_device(inputs, conv_early, conv_late, cotangent):
    owned = cotangent.shape[0]
    core = lax.axis_index("core")
    sent = inputs.reshape(inputs.shape[0] // owned, owned, inputs.shape[1], SIDE * SIDE, LANES)
    received = lax.all_to_all(sent, ("y", "xh"), split_axis=0, concat_axis=0, tiled=True)
    signal = cotangent.reshape(owned, SIDE * SIDE, SIDE, LANES).swapaxes(0, 1).reshape(CELLS, LANES)
    taps_late = conv_late.reshape(9, 3 * LANES, LANES)
    hidden, volume, slope_early = early_layer(received, conv_early.reshape(16, 2 * LANES, LANES))
    activated, late, late_sent, error = late_layer(core.reshape(1), hidden, taps_late, signal)
    late_other = swapped(late_sent)
    early, early_sent = backward(core.reshape(1), taps_late, volume, error, slope_early)
    shares = summed(core, early, swapped(early_sent), late, late_other)
    other = swapped(shares)
    early_total, late_total = placed(1 - core, other, placed(core, shares))
    return (
        activated.reshape(cotangent.shape),
        early_total.reshape(conv_early.shape),
        late_total.reshape(conv_late.shape),
    )


def solution(mesh):
    fine = jax.sharding.Mesh(mesh.devices.reshape(2, 4, 2, 4, 2), FINE)
    batch = ("xl", "z", "core")
    every = FINE
    return jax.shard_map(
        per_device,
        mesh=fine,
        in_specs=(
            P(batch, "y", "xh", None, None),
            P(),
            P(),
            P(every, None, None, None, None),
        ),
        out_specs=(P(every, None, None, None, None), P(), P()),
        check_vma=False,
    )
```

```python
import functools

import jax
import jax.numpy as jnp
from jax import lax
from jax.experimental import pallas as pl
from jax.experimental.pallas import tpu as pltpu
from jax.sharding import PartitionSpec as P

FINE = ("xl", "z", "core", "y", "xh")
BF16 = jnp.bfloat16
F32 = jnp.float32
SIDE = 8
LANES = 128
CELLS = SIDE * SIDE * 16
HALF = 4 * 4 * 4 * 64 // 2
HALF_LATE = 3 * 3 * 3 * 128 // 2
GRANULE = HALF_LATE // 9
SHARE = HALF // 64
RING = 4


def shifted(rows, by, lane=None):
    moved = pltpu.roll(rows, by % SIDE, 1)
    width = lax.broadcasted_iota(jnp.int32, rows.shape, 1)
    return jnp.where(width == (0 if by == 1 else SIDE - 1), 0.0, moved)


def three_widths(rows):
    return jnp.concatenate([shifted(rows, 1), rows, shifted(rows, -1)], axis=-1)


def clear_rim(ref, size):
    lanes = ref.shape[-1]
    slab = jnp.zeros((size, 16, lanes), BF16)
    ref[0] = slab
    ref[size - 1] = slab
    ref[:, 0] = slab
    ref[:, size - 1] = slab


def cube_conv(field, blocks, total):
    def product(first, count, weights, transposed):
        rows = jnp.concatenate([field[first : first + count, kh : kh + SIDE] for kh in range(3)], axis=-1)
        dims = (((1,), (1 if transposed else 0,)), ((), ()))
        return lax.dot_general(
            rows.reshape(count * LANES, 9 * LANES), weights, dims, preferred_element_type=F32
        )

    (first, transposed), (second, _), (third, _) = (blocks(kd) for kd in range(3))
    two = product(0, 9, jnp.concatenate([first, second], axis=0 if transposed else 1), transposed)
    total[...] = two[0:CELLS, 0:LANES] + two[LANES : LANES + CELLS, LANES:]
    total[...] += product(2, SIDE, third, transposed)


def early_kernel(received, conv_early, hidden, volume, slope_early, total):
    depth_blocks, height_blocks = 4, 2
    blank = jnp.zeros((9, 16, 2 * LANES), BF16)
    for dp in range(2):
        for hp in range(2):
            volume[2 * dp + hp, 0 if dp else 8] = blank
            volume[2 * dp + hp, :, 0 if hp else 8] = blank

    for block in range(depth_blocks * height_blocks):
        db, hb = divmod(block, height_blocks)
        for layer in range(4):
            half, dp = layer // 2, layer % 2
            samples = [
                received[block, s, layer].astype(F32).reshape(4, 2, SIDE, LANES) for s in range(2)
            ]
            for hp in range(2):
                centre = jnp.stack([x[:, hp] for x in samples], axis=1).reshape(8, SIDE, LANES)
                lane = lax.broadcasted_iota(jnp.int32, centre.shape, 2)
                sides = jnp.where(lane < LANES // 2, shifted(centre, -1), shifted(centre, 1))
                both = jnp.concatenate([centre, sides], axis=-1).reshape(4, 16, 2 * LANES)
                volume[2 * dp + hp, 2 * db + half + dp, 4 * hb + hp : 4 * hb + hp + 4] = both.astype(
                    BF16
                )

    def early_taps(kd, kh):
        tap = 4 * kd + kh
        return jnp.concatenate([conv_early[tap, 64:256], conv_early[tap, 0:64]], axis=0)

    for dp in range(2):
        rows = jnp.concatenate(
            [volume[2 * dp + (kh + 1) % 2, :, kh // 2 : kh // 2 + SIDE] for kh in range(4)], axis=-1
        )
        weights = [
            jnp.concatenate([early_taps(kd, kh) for kh in range(4)], axis=0) for kd in (1 - dp, 3 - dp)
        ]
        two = jnp.dot(
            rows.reshape(9 * LANES, 8 * LANES),
            jnp.concatenate(weights, axis=1),
            preferred_element_type=F32,
        )
        both = two[0:CELLS, 0:LANES] + two[LANES : LANES + CELLS, LANES:]
        if dp:
            total[...] += both
        else:
            total[...] = both

    clear_rim(hidden, 10)
    for d in range(SIDE):
        rows = pl.ds(d * LANES, LANES)
        early = total[rows]
        sigma = jax.nn.sigmoid(early)
        slope_early[rows] = sigma * (1.0 + early * (1.0 - sigma))
        value = (early * sigma).reshape(16, SIDE, LANES)
        hidden[d + 1, 1:9] = three_widths(value).reshape(SIDE, 16, 3 * LANES).astype(BF16)


def late_kernel(
    core, hidden, conv_late, cotangent, activated, kept, sent, error, hidden_t, total, grads
):
    def late_block(kd):
        return conv_late[3 * kd : 3 * kd + 3].reshape(9 * LANES, LANES), False

    cube_conv(hidden, late_block, total)

    clear_rim(error, 10)
    for d in range(SIDE):
        rows = pl.ds(d * LANES, LANES)
        late = total[rows]
        sigma = jax.nn.sigmoid(late)
        out = (late * sigma).reshape(SIDE, 2, SIDE, LANES)
        for s in range(2):
            activated[s, d] = out[:, s].reshape(SIDE * SIDE, LANES).astype(BF16)
        value = (cotangent[rows].astype(F32) * (sigma * (1.0 + late * (1.0 - sigma)))).reshape(16, SIDE, LANES)
        error[d + 1, 1:9] = three_widths(value).reshape(SIDE, 16, 3 * LANES).astype(BF16)

    grads[:, HALF_LATE:] = jnp.zeros((2, HALF - HALF_LATE, LANES), BF16)
    for d in range(SIDE):
        hidden_t[:, d * LANES : (d + 1) * LANES] = hidden[d + 1, 1:9].reshape(LANES, 3 * LANES).T

    for kh in range(3):
        for depth_taps in ((0, 1), (2,)):
            moved = [
                error[2 - kd : 10 - kd, 2 - kh : 10 - kh, :, LANES : 2 * LANES].reshape(CELLS, LANES)
                for kd in depth_taps
            ]
            side = moved[0] if len(moved) == 1 else jnp.concatenate(moved, axis=1)
            grad = jnp.dot(hidden_t[...], side, preferred_element_type=F32).astype(BF16)
            for column, kd in enumerate(depth_taps):
                for part in range(2):
                    half, granule = divmod(2 * (3 * kd + kh) + part, 9)
                    grads[
                        jnp.where(core[0] == half, 0, 1), granule * GRANULE : (granule + 1) * GRANULE
                    ] = grad[part * GRANULE : (part + 1) * GRANULE, column * LANES : (column + 1) * LANES]
    kept[...] = grads[0]
    sent[...] = grads[1]


def backward_kernel(
    core, conv_late, volume, error, slope_early, kept, sent, volume_t, error_early, total, grads
):
    clear_rim(error_early, 10)

    def back_block(kd):
        taps = [
            conv_late[3 * (2 - kd) + 2 - kh, (2 - kw) * LANES : (3 - kw) * LANES]
            for kh in range(3)
            for kw in range(3)
        ]
        return jnp.concatenate(taps, axis=1), True

    cube_conv(error, back_block, total)

    for d in range(SIDE):
        rows = pl.ds(d * LANES, LANES)
        value = total[rows].astype(BF16).astype(F32) * slope_early[rows]
        error_early[d + 1, 1:9] = value.astype(BF16).reshape(SIDE, 16, LANES)

    for phase in range(4):
        dp, hp = phase // 2, phase % 2
        for d in range(SIDE):
            volume_t[phase, :, d * LANES : (d + 1) * LANES] = (
                volume[phase, d + dp, hp : hp + SIDE].reshape(LANES, 2 * LANES).T
            )
    for phase in range(4):
        dp, hp = phase // 2, phase % 2
        for first in range(2):
            depth = dp + 1 - first
            moved = [
                error_early[depth : depth + SIDE, hp + 1 - second : hp + 1 - second + SIDE].reshape(
                    CELLS, LANES
                )
                for second in range(2)
            ]
            grad = jnp.dot(
                volume_t[phase], jnp.concatenate(moved, axis=1), preferred_element_type=F32
            ).astype(BF16)
            keep = jnp.where(core[0] == first, 0, 1)
            for second in range(2):
                tap = 4 * (2 * first + 1 - dp) + 2 * second + 1 - hp
                lanes = slice(second * LANES, (second + 1) * LANES)
                at = (tap - 8 * first) * 2 * LANES
                grads[keep, at + 64 : at + 256] = grad[0:192, lanes]
                grads[keep, at : at + 64] = grad[192:256, lanes]
    kept[...] = grads[0]
    sent[...] = grads[1]


VMEM = pl.BlockSpec(memory_space=pltpu.VMEM)
SMEM = pl.BlockSpec(memory_space=pltpu.SMEM)
ANY = pl.BlockSpec(memory_space=pl.ANY)
SMALL = pltpu.CompilerParams(vmem_limit_bytes=12 * 1024 * 1024)
LIMIT = pltpu.CompilerParams(vmem_limit_bytes=24 * 1024 * 1024)
VOLUME = (4, 9, 9, 16, 2 * LANES)
FIELD = (10, 10, 16, 3 * LANES)


HALF_ROWS = jax.ShapeDtypeStruct((HALF, LANES), BF16)


def cost(products, transcendentals=0):
    return pl.CostEstimate(
        flops=2 * CELLS * LANES * products,
        bytes_accessed=8 * 1024 * 1024,
        transcendentals=transcendentals,
    )


def early_layer(received, conv_early):
    return pl.pallas_call(
        early_kernel,
        out_shape=(
            jax.ShapeDtypeStruct(FIELD, BF16),
            jax.ShapeDtypeStruct(VOLUME, BF16),
            jax.ShapeDtypeStruct((CELLS, LANES), F32),
        ),
        in_specs=[VMEM, VMEM],
        out_specs=(VMEM,) * 3,
        scratch_shapes=[pltpu.VMEM((CELLS, LANES), F32)],
        compiler_params=LIMIT,
        cost_estimate=cost(16 * 256, CELLS * LANES),
    )(received, conv_early)


def late_layer(core, hidden, conv_late, cotangent):
    return pl.pallas_call(
        late_kernel,
        out_shape=(
            jax.ShapeDtypeStruct((2, SIDE, SIDE * SIDE, LANES), BF16),
            HALF_ROWS,
            HALF_ROWS,
            jax.ShapeDtypeStruct(FIELD, BF16),
        ),
        in_specs=[SMEM, VMEM, VMEM, VMEM],
        out_specs=(VMEM,) * 4,
        scratch_shapes=[
            pltpu.VMEM((3 * LANES, CELLS), BF16),
            pltpu.VMEM((CELLS, LANES), F32),
            pltpu.VMEM((2, HALF, LANES), BF16),
        ],
        compiler_params=LIMIT,
        cost_estimate=cost(2 * 27 * LANES, CELLS * LANES),
    )(core, hidden, conv_late, cotangent)


def backward(core, conv_late, volume, error, slope_early):
    return pl.pallas_call(
        backward_kernel,
        out_shape=(HALF_ROWS, HALF_ROWS),
        in_specs=[SMEM, VMEM, VMEM, VMEM, VMEM],
        out_specs=(VMEM, VMEM),
        scratch_shapes=[
            pltpu.VMEM((4, 2 * LANES, CELLS), BF16),
            pltpu.VMEM((10, 10, 16, LANES), BF16),
            pltpu.VMEM((CELLS, LANES), F32),
            pltpu.VMEM((2, HALF, LANES), BF16),
        ],
        compiler_params=LIMIT,
        cost_estimate=cost(16 * 256 + 27 * LANES),
    )(core, conv_late, volume, error, slope_early)


def ring_place(core):
    return jnp.where(core == 0, lax.axis_index("z"), lax.axis_index("y"))


def chip_routes():
    shifts = [[], [], [], []]
    planes = {}
    for xl in range(2):
        for z in range(RING):
            for core in range(2):
                for y in range(RING):
                    for xh in range(2):
                        index = lambda z, y: (((xl * RING + z) * 2 + core) * RING + y) * 2 + xh
                        for by, pairs in enumerate(shifts):
                            to = ((z + by) % RING, y) if core == 0 else (z, (y + by) % RING)
                            pairs.append((index(z, y), index(*to)))
                        planes.setdefault((core, z if core == 0 else y), []).append(index(z, y))
    return shifts, [planes[key] for key in sorted(planes)]


def pair_kernel(place, early, early_other, late, late_other, *blocks):
    rows = HALF // RING
    for n, block in enumerate(blocks):
        start = ((place[0] + n) % RING) * rows
        for kept, other, first in ((early, early_other, 0), (late, late_other, SHARE)):
            part = pl.ds(pl.multiple_of(start, rows), rows)
            value = (kept[part].astype(F32) + other[part].astype(F32)).astype(BF16)
            block[:, first : first + SHARE] = value.reshape(16, SHARE, LANES)


def pair_sums(place, early, early_other, late, late_other):
    block = jax.ShapeDtypeStruct((16, 2 * SHARE, LANES), BF16)
    return pl.pallas_call(
        pair_kernel,
        out_shape=(block,) * RING,
        in_specs=[SMEM] + [VMEM] * 4,
        out_specs=(VMEM,) * RING,
        compiler_params=SMALL,
        cost_estimate=pl.CostEstimate(flops=0, bytes_accessed=4 * 1024 * 1024, transcendentals=0),
    )(place.reshape(1), early, early_other, late, late_other)


def swapped(block):
    return lax.ppermute(block, "core", [(0, 1), (1, 0)])


def summed(core, early, early_other, late, late_other):
    shifts, planes = chip_routes()
    exchange = lambda blocks, groups: lax.all_to_all(
        blocks, FINE, split_axis=0, concat_axis=0, axis_index_groups=groups, tiled=True
    )
    blocks = pair_sums(ring_place(core), early, early_other, late, late_other)
    total = blocks[0].astype(F32)
    for by in range(1, RING):
        total += lax.ppermute(blocks[by], FINE, shifts[by]).astype(F32)
    shares = exchange(total.astype(BF16), planes)
    share = jnp.sum(shares.astype(F32), axis=0).astype(BF16)
    quarter = exchange(jnp.broadcast_to(share[None], (16,) + share.shape), planes)
    return [quarter] + [lax.ppermute(quarter, FINE, shifts[by]) for by in range(1, RING)]


def place_kernel(shifts, where, *refs):
    early, late, wide_early, wide_late, sems = refs[-5:]
    rows = HALF // RING
    last = HALF_LATE - 3 * rows
    copies = []
    for n in range(2 * len(shifts)):
        other, shift = n % 2, shifts[n // 2]
        half = where[0] ^ other
        quarter = (where[1 + other] - shift + RING) % RING
        piece = refs[n]
        wide_early[n] = piece[:, :SHARE].astype(F32).reshape(rows, LANES)
        wide_late[n] = piece[:, SHARE:].astype(F32).reshape(rows, LANES)
        at_early = pl.multiple_of(half * HALF + quarter * rows, rows)
        at_late = pl.multiple_of(half * HALF_LATE + quarter * rows, 64)
        to_early = pltpu.make_async_copy(wide_early.at[n], early.at[pl.ds(at_early, rows)], sems.at[n, 0])
        to_late = pltpu.make_async_copy(wide_late.at[n], late.at[pl.ds(at_late, rows)], sems.at[n, 1])
        to_end = pltpu.make_async_copy(
            wide_late.at[n, pl.ds(0, last)], late.at[pl.ds(at_late, last)], sems.at[n, 1]
        )
        to_early.start()
        pl.when(quarter < RING - 1)(to_late.start)
        pl.when(quarter == RING - 1)(to_end.start)
        copies.append((quarter, to_early, to_late, to_end))
    for quarter, to_early, to_late, to_end in copies:
        to_early.wait()
        pl.when(quarter < RING - 1)(to_late.wait)
        pl.when(quarter == RING - 1)(to_end.wait)


def placed(where, shifts, pieces, so_far):
    count = len(pieces)
    return pl.pallas_call(
        functools.partial(place_kernel, shifts),
        out_shape=(
            jax.ShapeDtypeStruct((2 * HALF, LANES), F32),
            jax.ShapeDtypeStruct((2 * HALF_LATE, LANES), F32),
        ),
        in_specs=[SMEM] + [VMEM] * count + [ANY] * len(so_far),
        out_specs=(ANY, ANY),
        input_output_aliases={1 + count + n: n for n in range(len(so_far))},
        scratch_shapes=[
            pltpu.VMEM((count, HALF // RING, LANES), F32),
            pltpu.VMEM((count, HALF // RING, LANES), F32),
            pltpu.SemaphoreType.DMA((count, 2)),
        ],
        compiler_params=SMALL,
        cost_estimate=pl.CostEstimate(flops=0, bytes_accessed=count * 768 * 1024, transcendentals=0),
    )(where, *pieces, *so_far)


def per_device(inputs, conv_early, conv_late, cotangent):
    owned = cotangent.shape[0]
    core = lax.axis_index("core")
    sent = inputs.reshape(inputs.shape[0] // owned, owned, inputs.shape[1], SIDE * SIDE, LANES)
    received = lax.all_to_all(sent, ("y", "xh"), split_axis=0, concat_axis=0, tiled=True)
    signal = cotangent.reshape(owned, SIDE * SIDE, SIDE, LANES).swapaxes(0, 1).reshape(CELLS, LANES)
    taps_late = conv_late.reshape(9, 3 * LANES, LANES)
    hidden, volume, slope_early = early_layer(received, conv_early.reshape(16, 2 * LANES, LANES))
    activated, late, late_sent, error = late_layer(core.reshape(1), hidden, taps_late, signal)
    late_other = swapped(late_sent)
    early, early_sent = backward(core.reshape(1), taps_late, volume, error, slope_early)
    pieces = summed(core, early, swapped(early_sent), late, late_other)
    where = jnp.stack([core, ring_place(core), ring_place(1 - core)])
    totals = placed(where, (0,), [pieces[0], swapped(pieces[0])], ())
    *totals, one, three = lax.optimization_barrier((*totals, pieces[1], pieces[3]))
    totals = placed(where, (1, 3), [one, swapped(one), three, swapped(three)], totals)
    early_total, late_total = placed(where, (2,), [pieces[2], swapped(pieces[2])], totals)
    return (
        activated.reshape(cotangent.shape),
        early_total.reshape(conv_early.shape),
        late_total.reshape(conv_late.shape),
    )


def solution(mesh):
    fine = jax.sharding.Mesh(mesh.devices.reshape(2, 4, 2, 4, 2), FINE)
    batch = ("xl", "z", "core")
    every = FINE
    return jax.shard_map(
        per_device,
        mesh=fine,
        in_specs=(
            P(batch, "y", "xh", None, None),
            P(),
            P(),
            P(every, None, None, None, None),
        ),
        out_specs=(P(every, None, None, None, None), P(), P()),
        check_vma=False,
    )
```

```python
import functools

import jax
import jax.numpy as jnp
from jax import lax
from jax.experimental import pallas as pl
from jax.experimental.pallas import tpu as pltpu
from jax.sharding import PartitionSpec as P

FINE = ("xl", "z", "core", "y", "xh")
BF16 = jnp.bfloat16
F32 = jnp.float32
SIDE = 8
LANES = 128
CELLS = SIDE * SIDE * 16
HALF = 4 * 4 * 4 * 64 // 2
HALF_LATE = 3 * 3 * 3 * 128 // 2
GRANULE = HALF_LATE // 9
SHARE = HALF // 64
SHARE_LATE = HALF_LATE // 64
RING = 4
QUARTER = HALF // RING
QUARTER_LATE = HALF_LATE // RING


def shifted(rows, by, lane=None):
    moved = pltpu.roll(rows, by % SIDE, 1)
    width = lax.broadcasted_iota(jnp.int32, rows.shape, 1)
    return jnp.where(width == (0 if by == 1 else SIDE - 1), 0.0, moved)


def three_widths(rows):
    return jnp.concatenate([shifted(rows, 1), rows, shifted(rows, -1)], axis=-1)


def clear_rim(ref, size):
    lanes = ref.shape[-1]
    slab = jnp.zeros((size, 16, lanes), BF16)
    ref[0] = slab
    ref[size - 1] = slab
    ref[:, 0] = slab
    ref[:, size - 1] = slab


def cube_conv(field, blocks, total):
    def product(first, count, weights, transposed):
        rows = jnp.concatenate([field[first : first + count, kh : kh + SIDE] for kh in range(3)], axis=-1)
        dims = (((1,), (1 if transposed else 0,)), ((), ()))
        return lax.dot_general(
            rows.reshape(count * LANES, 9 * LANES), weights, dims, preferred_element_type=F32
        )

    (first, transposed), (second, _), (third, _) = (blocks(kd) for kd in range(3))
    two = product(0, 9, jnp.concatenate([first, second], axis=0 if transposed else 1), transposed)
    total[...] = two[0:CELLS, 0:LANES] + two[LANES : LANES + CELLS, LANES:]
    total[...] += product(2, SIDE, third, transposed)


def early_kernel(received, conv_early, hidden, volume, slope_early, total):
    depth_blocks, height_blocks = 4, 2
    blank = jnp.zeros((9, 16, 2 * LANES), BF16)
    for dp in range(2):
        for hp in range(2):
            volume[2 * dp + hp, 0 if dp else 8] = blank
            volume[2 * dp + hp, :, 0 if hp else 8] = blank

    for block in range(depth_blocks * height_blocks):
        db, hb = divmod(block, height_blocks)
        for layer in range(4):
            half, dp = layer // 2, layer % 2
            samples = [
                received[block, s, layer].astype(F32).reshape(4, 2, SIDE, LANES) for s in range(2)
            ]
            for hp in range(2):
                centre = jnp.stack([x[:, hp] for x in samples], axis=1).reshape(8, SIDE, LANES)
                lane = lax.broadcasted_iota(jnp.int32, centre.shape, 2)
                sides = jnp.where(lane < LANES // 2, shifted(centre, -1), shifted(centre, 1))
                both = jnp.concatenate([centre, sides], axis=-1).reshape(4, 16, 2 * LANES)
                volume[2 * dp + hp, 2 * db + half + dp, 4 * hb + hp : 4 * hb + hp + 4] = both.astype(
                    BF16
                )

    def early_taps(kd, kh):
        tap = 4 * kd + kh
        return jnp.concatenate([conv_early[tap, 64:256], conv_early[tap, 0:64]], axis=0)

    for dp in range(2):
        rows = jnp.concatenate(
            [volume[2 * dp + (kh + 1) % 2, :, kh // 2 : kh // 2 + SIDE] for kh in range(4)], axis=-1
        )
        weights = [
            jnp.concatenate([early_taps(kd, kh) for kh in range(4)], axis=0) for kd in (1 - dp, 3 - dp)
        ]
        two = jnp.dot(
            rows.reshape(9 * LANES, 8 * LANES),
            jnp.concatenate(weights, axis=1),
            preferred_element_type=F32,
        )
        both = two[0:CELLS, 0:LANES] + two[LANES : LANES + CELLS, LANES:]
        if dp:
            total[...] += both
        else:
            total[...] = both

    clear_rim(hidden, 10)
    for d in range(SIDE):
        rows = pl.ds(d * LANES, LANES)
        early = total[rows]
        sigma = jax.nn.sigmoid(early)
        slope_early[rows] = sigma * (1.0 + early * (1.0 - sigma))
        value = (early * sigma).reshape(16, SIDE, LANES)
        hidden[d + 1, 1:9] = three_widths(value).reshape(SIDE, 16, 3 * LANES).astype(BF16)


def late_kernel(
    core, hidden, conv_late, cotangent, activated, kept, sent, error, hidden_t, total, grads
):
    def late_block(kd):
        return conv_late[3 * kd : 3 * kd + 3].reshape(9 * LANES, LANES), False

    cube_conv(hidden, late_block, total)

    clear_rim(error, 10)
    for d in range(SIDE):
        rows = pl.ds(d * LANES, LANES)
        late = total[rows]
        sigma = jax.nn.sigmoid(late)
        out = (late * sigma).reshape(SIDE, 2, SIDE, LANES)
        for s in range(2):
            activated[s, d] = out[:, s].reshape(SIDE * SIDE, LANES).astype(BF16)
        value = (cotangent[rows].astype(F32) * (sigma * (1.0 + late * (1.0 - sigma)))).reshape(16, SIDE, LANES)
        error[d + 1, 1:9] = three_widths(value).reshape(SIDE, 16, 3 * LANES).astype(BF16)

    for d in range(SIDE):
        hidden_t[:, d * LANES : (d + 1) * LANES] = hidden[d + 1, 1:9].reshape(LANES, 3 * LANES).T

    for kh in range(3):
        for depth_taps in ((0, 1), (2,)):
            moved = [
                error[2 - kd : 10 - kd, 2 - kh : 10 - kh, :, LANES : 2 * LANES].reshape(CELLS, LANES)
                for kd in depth_taps
            ]
            side = moved[0] if len(moved) == 1 else jnp.concatenate(moved, axis=1)
            grad = jnp.dot(hidden_t[...], side, preferred_element_type=F32).astype(BF16)
            for column, kd in enumerate(depth_taps):
                for part in range(2):
                    half, granule = divmod(2 * (3 * kd + kh) + part, 9)
                    grads[
                        jnp.where(core[0] == half, 0, 1), granule * GRANULE : (granule + 1) * GRANULE
                    ] = grad[part * GRANULE : (part + 1) * GRANULE, column * LANES : (column + 1) * LANES]
    kept[...] = grads[0]
    sent[...] = grads[1]


def backward_kernel(conv_late, volume, error, slope_early, error_early, volume_t, total):
    clear_rim(error_early, 10)

    def back_block(kd):
        taps = [
            conv_late[3 * (2 - kd) + 2 - kh, (2 - kw) * LANES : (3 - kw) * LANES]
            for kh in range(3)
            for kw in range(3)
        ]
        return jnp.concatenate(taps, axis=1), True

    cube_conv(error, back_block, total)

    for d in range(SIDE):
        rows = pl.ds(d * LANES, LANES)
        value = total[rows].astype(BF16).astype(F32) * slope_early[rows]
        error_early[d + 1, 1:9] = value.astype(BF16).reshape(SIDE, 16, LANES)

    for phase in range(4):
        dp, hp = phase // 2, phase % 2
        for d in range(SIDE):
            volume_t[phase, :, d * LANES : (d + 1) * LANES] = (
                volume[phase, d + dp, hp : hp + SIDE].reshape(LANES, 2 * LANES).T
            )


def early_grad_kernel(core, error_early, volume_t, late, late_other, kept, sent, late_sum, grads):
    late_sum[...] = (late[...].astype(F32) + late_other[...].astype(F32)).astype(BF16)
    for phase in range(4):
        dp, hp = phase // 2, phase % 2
        for first in range(2):
            depth = dp + 1 - first
            moved = [
                error_early[depth : depth + SIDE, hp + 1 - second : hp + 1 - second + SIDE].reshape(
                    CELLS, LANES
                )
                for second in range(2)
            ]
            grad = jnp.dot(
                volume_t[phase], jnp.concatenate(moved, axis=1), preferred_element_type=F32
            ).astype(BF16)
            keep = jnp.where(core[0] == first, 0, 1)
            for second in range(2):
                tap = 4 * (2 * first + 1 - dp) + 2 * second + 1 - hp
                lanes = slice(second * LANES, (second + 1) * LANES)
                at = (tap - 8 * first) * 2 * LANES
                grads[keep, at + 64 : at + 256] = grad[0:192, lanes]
                grads[keep, at : at + 64] = grad[192:256, lanes]
    kept[...] = grads[0]
    sent[...] = grads[1]


VMEM = pl.BlockSpec(memory_space=pltpu.VMEM)
SMEM = pl.BlockSpec(memory_space=pltpu.SMEM)
ANY = pl.BlockSpec(memory_space=pl.ANY)
SMALL = pltpu.CompilerParams(vmem_limit_bytes=12 * 1024 * 1024)
LIMIT = pltpu.CompilerParams(vmem_limit_bytes=24 * 1024 * 1024)
VOLUME = (4, 9, 9, 16, 2 * LANES)
FIELD = (10, 10, 16, 3 * LANES)


EARLY_ROWS = jax.ShapeDtypeStruct((HALF, LANES), BF16)
LATE_ROWS = jax.ShapeDtypeStruct((HALF_LATE, LANES), BF16)


def cost(products, transcendentals=0):
    return pl.CostEstimate(
        flops=2 * CELLS * LANES * products,
        bytes_accessed=8 * 1024 * 1024,
        transcendentals=transcendentals,
    )


def early_layer(received, conv_early):
    return pl.pallas_call(
        early_kernel,
        out_shape=(
            jax.ShapeDtypeStruct(FIELD, BF16),
            jax.ShapeDtypeStruct(VOLUME, BF16),
            jax.ShapeDtypeStruct((CELLS, LANES), F32),
        ),
        in_specs=[VMEM, VMEM],
        out_specs=(VMEM,) * 3,
        scratch_shapes=[pltpu.VMEM((CELLS, LANES), F32)],
        compiler_params=LIMIT,
        cost_estimate=cost(16 * 256, CELLS * LANES),
    )(received, conv_early)


def late_layer(core, hidden, conv_late, cotangent):
    return pl.pallas_call(
        late_kernel,
        out_shape=(
            jax.ShapeDtypeStruct((2, SIDE, SIDE * SIDE, LANES), BF16),
            LATE_ROWS,
            LATE_ROWS,
            jax.ShapeDtypeStruct(FIELD, BF16),
        ),
        in_specs=[SMEM, VMEM, VMEM, VMEM],
        out_specs=(VMEM,) * 4,
        scratch_shapes=[
            pltpu.VMEM((3 * LANES, CELLS), BF16),
            pltpu.VMEM((CELLS, LANES), F32),
            pltpu.VMEM((2, HALF_LATE, LANES), BF16),
        ],
        compiler_params=LIMIT,
        cost_estimate=cost(2 * 27 * LANES, CELLS * LANES),
    )(core, hidden, conv_late, cotangent)


def backward(conv_late, volume, error, slope_early):
    return pl.pallas_call(
        backward_kernel,
        out_shape=(
            jax.ShapeDtypeStruct((10, 10, 16, LANES), BF16),
            jax.ShapeDtypeStruct((4, 2 * LANES, CELLS), BF16),
        ),
        in_specs=[VMEM] * 4,
        out_specs=(VMEM, VMEM),
        scratch_shapes=[pltpu.VMEM((CELLS, LANES), F32)],
        compiler_params=LIMIT,
        cost_estimate=cost(27 * LANES),
    )(conv_late, volume, error, slope_early)


def early_grad(core, error_early, volume_t, late, late_other):
    return pl.pallas_call(
        early_grad_kernel,
        out_shape=(EARLY_ROWS, EARLY_ROWS, LATE_ROWS),
        in_specs=[SMEM] + [VMEM] * 4,
        out_specs=(VMEM,) * 3,
        scratch_shapes=[pltpu.VMEM((2, HALF, LANES), BF16)],
        compiler_params=LIMIT,
        cost_estimate=cost(16 * 256),
    )(core, error_early, volume_t, late, late_other)


def ring_place(core):
    return jnp.where(core == 0, lax.axis_index("z"), lax.axis_index("y"))


def chip_routes():
    shifts = [[], [], [], []]
    planes = {}
    for xl in range(2):
        for z in range(RING):
            for core in range(2):
                for y in range(RING):
                    for xh in range(2):
                        index = lambda z, y: (((xl * RING + z) * 2 + core) * RING + y) * 2 + xh
                        for by, pairs in enumerate(shifts):
                            to = ((z + by) % RING, y) if core == 0 else (z, (y + by) % RING)
                            pairs.append((index(z, y), index(*to)))
                        planes.setdefault((core, z if core == 0 else y), []).append(index(z, y))
    return shifts, [planes[key] for key in sorted(planes)]


def small_call(kernel, out_shape, scratch, *args):
    return pl.pallas_call(
        kernel,
        out_shape=out_shape,
        in_specs=[SMEM if arg.ndim == 1 else VMEM for arg in args],
        out_specs=jax.tree.map(lambda _: VMEM, out_shape),
        scratch_shapes=scratch,
        compiler_params=SMALL,
        cost_estimate=pl.CostEstimate(flops=0, bytes_accessed=2 * 1024 * 1024, transcendentals=0),
    )(*args)


def pair_kernel(place, early, early_other, late_sum, *blocks):
    for n, block in enumerate(blocks):
        quarter = (place[0] + n) % RING
        part = pl.ds(pl.multiple_of(quarter * QUARTER, QUARTER), QUARTER)
        block[:QUARTER] = (early[part].astype(F32) + early_other[part].astype(F32)).astype(BF16)
        block[QUARTER:] = late_sum[pl.ds(pl.multiple_of(quarter * QUARTER_LATE, 16), QUARTER_LATE)]


def pair_sums(place, early, early_other, late_sum):
    block = jax.ShapeDtypeStruct((QUARTER + QUARTER_LATE, LANES), BF16)
    return small_call(pair_kernel, (block,) * RING, [], place.reshape(1), early, early_other, late_sum)


def ring_kernel(first, second, third, fourth, shares, late):
    total = first[...].astype(F32) + second[...].astype(F32)
    total = total + third[...].astype(F32) + fourth[...].astype(F32)
    shares[:, :SHARE] = total[:QUARTER].astype(BF16).reshape(16, SHARE, LANES)
    late[:QUARTER_LATE] = total[QUARTER:]
    late[QUARTER_LATE:] = jnp.zeros((late.shape[0] - QUARTER_LATE, LANES), F32)
    for n in range(16):
        shares[n, SHARE:] = late[n * SHARE_LATE : n * SHARE_LATE + SHARE].astype(BF16)


def share_kernel(shares, spread):
    total = jnp.sum(shares[...].astype(F32), axis=0).astype(BF16)
    for n in range(16):
        spread[n] = total


def join_kernel(shares, rows, late):
    rows[:QUARTER] = shares[:, :SHARE].reshape(QUARTER, LANES)
    for n in range(16):
        late[n * SHARE_LATE : n * SHARE_LATE + SHARE] = shares[n, SHARE:].astype(F32)
    rows[QUARTER:] = late[:QUARTER_LATE].astype(BF16)


def swapped(block):
    return lax.ppermute(block, "core", [(0, 1), (1, 0)])


def summed(core, early, early_other, late_sum):
    shifts, planes = chip_routes()
    exchange = lambda blocks: lax.all_to_all(
        blocks, FINE, split_axis=0, concat_axis=0, axis_index_groups=planes, tiled=True
    )
    blocks = list(pair_sums(ring_place(core), early, early_other, late_sum))
    for by in range(1, RING):
        blocks[by] = lax.ppermute(blocks[by], FINE, shifts[by])
    shares = jax.ShapeDtypeStruct((16, 2 * SHARE, LANES), BF16)
    uneven = [pltpu.VMEM((QUARTER_LATE + 8, LANES), F32)]
    sent = exchange(small_call(ring_kernel, shares, uneven, *blocks))
    spread = exchange(small_call(share_kernel, shares, [], sent))
    rows = jax.ShapeDtypeStruct((QUARTER + QUARTER_LATE, LANES), BF16)
    quarter = small_call(join_kernel, rows, uneven, spread)
    return [quarter] + [lax.ppermute(quarter, FINE, shifts[by]) for by in range(1, RING)]


def place_kernel(origins, where, *refs):
    early, late, wide, sems = refs[-4:]
    copies = []
    for n, (shift, other) in enumerate(origins):
        half = where[0] ^ other
        quarter = (where[1 + other] - shift + RING) % RING
        wide[n] = refs[n][...].astype(F32)
        at_early = pl.multiple_of(half * HALF + quarter * QUARTER, QUARTER)
        at_late = pl.multiple_of(half * HALF_LATE + quarter * QUARTER_LATE, 16)
        copies += [
            pltpu.make_async_copy(
                wide.at[n, pl.ds(0, QUARTER)], early.at[pl.ds(at_early, QUARTER)], sems.at[n, 0]
            ),
            pltpu.make_async_copy(
                wide.at[n, pl.ds(QUARTER, QUARTER_LATE)],
                late.at[pl.ds(at_late, QUARTER_LATE)],
                sems.at[n, 1],
            ),
        ]
        for copy in copies[-2:]:
            copy.start()
    for copy in copies:
        copy.wait()


def placed(where, origins, pieces, so_far):
    count = len(pieces)
    return pl.pallas_call(
        functools.partial(place_kernel, origins),
        out_shape=(
            jax.ShapeDtypeStruct((2 * HALF, LANES), F32),
            jax.ShapeDtypeStruct((2 * HALF_LATE, LANES), F32),
        ),
        in_specs=[SMEM] + [VMEM] * count + [ANY] * len(so_far),
        out_specs=(ANY, ANY),
        input_output_aliases={1 + count + n: n for n in range(len(so_far))},
        scratch_shapes=[
            pltpu.VMEM((count, QUARTER + QUARTER_LATE, LANES), F32),
            pltpu.SemaphoreType.DMA((count, 2)),
        ],
        compiler_params=SMALL,
        cost_estimate=pl.CostEstimate(flops=0, bytes_accessed=count * 768 * 1024, transcendentals=0),
    )(where, *pieces, *so_far)


def per_device(inputs, conv_early, conv_late, cotangent):
    owned = cotangent.shape[0]
    core = lax.axis_index("core")
    sent = inputs.reshape(inputs.shape[0] // owned, owned, inputs.shape[1], SIDE * SIDE, LANES)
    received = lax.all_to_all(sent, ("y", "xh"), split_axis=0, concat_axis=0, tiled=True)
    signal = cotangent.reshape(owned, SIDE * SIDE, SIDE, LANES).swapaxes(0, 1).reshape(CELLS, LANES)
    taps_late = conv_late.reshape(9, 3 * LANES, LANES)
    hidden, volume, slope_early = early_layer(received, conv_early.reshape(16, 2 * LANES, LANES))
    activated, late, late_sent, error = late_layer(core.reshape(1), hidden, taps_late, signal)
    late_other = swapped(late_sent)
    error_early, volume_t = backward(taps_late, volume, error, slope_early)
    early, early_sent, late_sum = early_grad(core.reshape(1), error_early, volume_t, late, late_other)
    zero, one, two, three = summed(core, early, swapped(early_sent), late_sum)
    where = jnp.stack([core, ring_place(core), ring_place(1 - core)])
    totals = placed(where, ((0, 0), (0, 1)), [zero, swapped(zero)], ())
    *totals, one, three = lax.optimization_barrier((*totals, one, three))
    swaps = [swapped(piece) for piece in (one, three, two)]
    totals = placed(where, ((1, 0), (3, 0)), [one, three], totals)
    early_total, late_total = placed(
        where, ((2, 0), (1, 1), (3, 1), (2, 1)), [two, *swaps], totals
    )
    return (
        activated.reshape(cotangent.shape),
        early_total.reshape(conv_early.shape),
        late_total.reshape(conv_late.shape),
    )


def solution(mesh):
    fine = jax.sharding.Mesh(mesh.devices.reshape(2, 4, 2, 4, 2), FINE)
    batch = ("xl", "z", "core")
    every = FINE
    return jax.shard_map(
        per_device,
        mesh=fine,
        in_specs=(
            P(batch, "y", "xh", None, None),
            P(),
            P(),
            P(every, None, None, None, None),
        ),
        out_specs=(P(every, None, None, None, None), P(), P()),
        check_vma=False,
    )
```

```python
import functools

import jax
import jax.numpy as jnp
from jax import lax
from jax.experimental import pallas as pl
from jax.experimental.pallas import tpu as pltpu
from jax.sharding import PartitionSpec as P

FINE = ("xl", "z", "core", "y", "xh")
BF16 = jnp.bfloat16
F32 = jnp.float32
SIDE = 8
LANES = 128
CELLS = SIDE * SIDE * 16
HALF = 4 * 4 * 4 * 64 // 2
HALF_LATE = 3 * 3 * 3 * 128 // 2
GRANULE = HALF_LATE // 9
SHARE = HALF // 64
SHARE_LATE = HALF_LATE // 64
RING = 4
QUARTER = HALF // RING
QUARTER_LATE = HALF_LATE // RING


def shifted(rows, by, lane=None):
    moved = pltpu.roll(rows, by % SIDE, 1)
    width = lax.broadcasted_iota(jnp.int32, rows.shape, 1)
    return jnp.where(width == (0 if by == 1 else SIDE - 1), 0.0, moved)


def three_widths(rows):
    return jnp.concatenate([shifted(rows, 1), rows, shifted(rows, -1)], axis=-1)


def clear_rim(ref, size):
    lanes = ref.shape[-1]
    slab = jnp.zeros((size, 16, lanes), BF16)
    ref[0] = slab
    ref[size - 1] = slab
    ref[:, 0] = slab
    ref[:, size - 1] = slab


def cube_conv(field, blocks, total):
    def product(first, count, weights, transposed):
        rows = jnp.concatenate([field[first : first + count, kh : kh + SIDE] for kh in range(3)], axis=-1)
        dims = (((1,), (1 if transposed else 0,)), ((), ()))
        return lax.dot_general(
            rows.reshape(count * LANES, 9 * LANES), weights, dims, preferred_element_type=F32
        )

    (first, transposed), (second, _), (third, _) = (blocks(kd) for kd in range(3))
    two = product(0, 9, jnp.concatenate([first, second], axis=0 if transposed else 1), transposed)
    total[...] = two[0:CELLS, 0:LANES] + two[LANES : LANES + CELLS, LANES:]
    total[...] += product(2, SIDE, third, transposed)


def early_kernel(received, conv_early, hidden, volume, slope_early, total):
    depth_blocks, height_blocks = 4, 2
    blank = jnp.zeros((9, 16, 2 * LANES), BF16)
    for dp in range(2):
        for hp in range(2):
            volume[2 * dp + hp, 0 if dp else 8] = blank
            volume[2 * dp + hp, :, 0 if hp else 8] = blank

    for block in range(depth_blocks * height_blocks):
        db, hb = divmod(block, height_blocks)
        for layer in range(4):
            half, dp = layer // 2, layer % 2
            samples = [
                received[block, s, layer].astype(F32).reshape(4, 2, SIDE, LANES) for s in range(2)
            ]
            for hp in range(2):
                centre = jnp.stack([x[:, hp] for x in samples], axis=1).reshape(8, SIDE, LANES)
                lane = lax.broadcasted_iota(jnp.int32, centre.shape, 2)
                sides = jnp.where(lane < LANES // 2, shifted(centre, -1), shifted(centre, 1))
                both = jnp.concatenate([centre, sides], axis=-1).reshape(4, 16, 2 * LANES)
                volume[2 * dp + hp, 2 * db + half + dp, 4 * hb + hp : 4 * hb + hp + 4] = both.astype(
                    BF16
                )

    def early_taps(kd, kh):
        tap = 4 * kd + kh
        return jnp.concatenate([conv_early[tap, 64:256], conv_early[tap, 0:64]], axis=0)

    for dp in range(2):
        rows = jnp.concatenate(
            [volume[2 * dp + (kh + 1) % 2, :, kh // 2 : kh // 2 + SIDE] for kh in range(4)], axis=-1
        )
        weights = [
            jnp.concatenate([early_taps(kd, kh) for kh in range(4)], axis=0) for kd in (1 - dp, 3 - dp)
        ]
        two = jnp.dot(
            rows.reshape(9 * LANES, 8 * LANES),
            jnp.concatenate(weights, axis=1),
            preferred_element_type=F32,
        )
        both = two[0:CELLS, 0:LANES] + two[LANES : LANES + CELLS, LANES:]
        if dp:
            total[...] += both
        else:
            total[...] = both

    clear_rim(hidden, 10)
    for d in range(SIDE):
        rows = pl.ds(d * LANES, LANES)
        early = total[rows]
        sigma = jax.nn.sigmoid(early)
        slope_early[rows] = sigma * (1.0 + early * (1.0 - sigma))
        value = (early * sigma).reshape(16, SIDE, LANES)
        hidden[d + 1, 1:9] = three_widths(value).reshape(SIDE, 16, 3 * LANES).astype(BF16)


def late_kernel(
    core, hidden, conv_late, cotangent, activated, kept, sent, error, hidden_t, total, grads
):
    def late_block(kd):
        return conv_late[3 * kd : 3 * kd + 3].reshape(9 * LANES, LANES), False

    cube_conv(hidden, late_block, total)

    clear_rim(error, 10)
    for d in range(SIDE):
        rows = pl.ds(d * LANES, LANES)
        late = total[rows]
        sigma = jax.nn.sigmoid(late)
        out = (late * sigma).reshape(SIDE, 2, SIDE, LANES)
        for s in range(2):
            activated[s, d] = out[:, s].reshape(SIDE * SIDE, LANES).astype(BF16)
        value = (cotangent[rows].astype(F32) * (sigma * (1.0 + late * (1.0 - sigma)))).reshape(16, SIDE, LANES)
        error[d + 1, 1:9] = three_widths(value).reshape(SIDE, 16, 3 * LANES).astype(BF16)

    for d in range(SIDE):
        hidden_t[:, d * LANES : (d + 1) * LANES] = hidden[d + 1, 1:9].reshape(LANES, 3 * LANES).T

    for kh in range(3):
        for depth_taps in ((0, 1), (2,)):
            moved = [
                error[2 - kd : 10 - kd, 2 - kh : 10 - kh, :, LANES : 2 * LANES].reshape(CELLS, LANES)
                for kd in depth_taps
            ]
            side = moved[0] if len(moved) == 1 else jnp.concatenate(moved, axis=1)
            grad = jnp.dot(hidden_t[...], side, preferred_element_type=F32).astype(BF16)
            for column, kd in enumerate(depth_taps):
                for part in range(2):
                    half, granule = divmod(2 * (3 * kd + kh) + part, 9)
                    grads[
                        jnp.where(core[0] == half, 0, 1), granule * GRANULE : (granule + 1) * GRANULE
                    ] = grad[part * GRANULE : (part + 1) * GRANULE, column * LANES : (column + 1) * LANES]
    kept[...] = grads[0]
    sent[...] = grads[1]


def backward_kernel(conv_late, volume, error, slope_early, error_early, volume_t, total):
    clear_rim(error_early, 10)

    def back_block(kd):
        taps = [
            conv_late[3 * (2 - kd) + 2 - kh, (2 - kw) * LANES : (3 - kw) * LANES]
            for kh in range(3)
            for kw in range(3)
        ]
        return jnp.concatenate(taps, axis=1), True

    cube_conv(error, back_block, total)

    for d in range(SIDE):
        rows = pl.ds(d * LANES, LANES)
        value = total[rows].astype(BF16).astype(F32) * slope_early[rows]
        error_early[d + 1, 1:9] = value.astype(BF16).reshape(SIDE, 16, LANES)

    for phase in range(4):
        dp, hp = phase // 2, phase % 2
        for d in range(SIDE):
            volume_t[phase, :, d * LANES : (d + 1) * LANES] = (
                volume[phase, d + dp, hp : hp + SIDE].reshape(LANES, 2 * LANES).T
            )


def early_grad_kernel(core, error_early, volume_t, late, late_other, kept, sent, late_sum, grads):
    late_sum[...] = (late[...].astype(F32) + late_other[...].astype(F32)).astype(BF16)
    for phase in range(4):
        dp, hp = phase // 2, phase % 2
        for first in range(2):
            depth = dp + 1 - first
            moved = [
                error_early[depth : depth + SIDE, hp + 1 - second : hp + 1 - second + SIDE].reshape(
                    CELLS, LANES
                )
                for second in range(2)
            ]
            grad = jnp.dot(
                volume_t[phase], jnp.concatenate(moved, axis=1), preferred_element_type=F32
            ).astype(BF16)
            keep = jnp.where(core[0] == first, 0, 1)
            for second in range(2):
                tap = 4 * (2 * first + 1 - dp) + 2 * second + 1 - hp
                lanes = slice(second * LANES, (second + 1) * LANES)
                at = (tap - 8 * first) * 2 * LANES
                grads[keep, at + 64 : at + 256] = grad[0:192, lanes]
                grads[keep, at : at + 64] = grad[192:256, lanes]
    kept[...] = grads[0]
    sent[...] = grads[1]


VMEM = pl.BlockSpec(memory_space=pltpu.VMEM)
SMEM = pl.BlockSpec(memory_space=pltpu.SMEM)
ANY = pl.BlockSpec(memory_space=pl.ANY)
SMALL = pltpu.CompilerParams(vmem_limit_bytes=12 * 1024 * 1024)
LIMIT = pltpu.CompilerParams(vmem_limit_bytes=24 * 1024 * 1024)
VOLUME = (4, 9, 9, 16, 2 * LANES)
FIELD = (10, 10, 16, 3 * LANES)


EARLY_ROWS = jax.ShapeDtypeStruct((HALF, LANES), BF16)
LATE_ROWS = jax.ShapeDtypeStruct((HALF_LATE, LANES), BF16)


def cost(products, transcendentals=0):
    return pl.CostEstimate(
        flops=2 * CELLS * LANES * products,
        bytes_accessed=8 * 1024 * 1024,
        transcendentals=transcendentals,
    )


def early_layer(received, conv_early):
    return pl.pallas_call(
        early_kernel,
        out_shape=(
            jax.ShapeDtypeStruct(FIELD, BF16),
            jax.ShapeDtypeStruct(VOLUME, BF16),
            jax.ShapeDtypeStruct((CELLS, LANES), F32),
        ),
        in_specs=[VMEM, VMEM],
        out_specs=(VMEM,) * 3,
        scratch_shapes=[pltpu.VMEM((CELLS, LANES), F32)],
        compiler_params=LIMIT,
        cost_estimate=cost(16 * 256, CELLS * LANES),
    )(received, conv_early)


def late_layer(core, hidden, conv_late, cotangent):
    return pl.pallas_call(
        late_kernel,
        out_shape=(
            jax.ShapeDtypeStruct((2, SIDE, SIDE * SIDE, LANES), BF16),
            LATE_ROWS,
            LATE_ROWS,
            jax.ShapeDtypeStruct(FIELD, BF16),
        ),
        in_specs=[SMEM, VMEM, VMEM, VMEM],
        out_specs=(VMEM,) * 4,
        scratch_shapes=[
            pltpu.VMEM((3 * LANES, CELLS), BF16),
            pltpu.VMEM((CELLS, LANES), F32),
            pltpu.VMEM((2, HALF_LATE, LANES), BF16),
        ],
        compiler_params=LIMIT,
        cost_estimate=cost(2 * 27 * LANES, CELLS * LANES),
    )(core, hidden, conv_late, cotangent)


def backward(conv_late, volume, error, slope_early):
    return pl.pallas_call(
        backward_kernel,
        out_shape=(
            jax.ShapeDtypeStruct((10, 10, 16, LANES), BF16),
            jax.ShapeDtypeStruct((4, 2 * LANES, CELLS), BF16),
        ),
        in_specs=[VMEM] * 4,
        out_specs=(VMEM, VMEM),
        scratch_shapes=[pltpu.VMEM((CELLS, LANES), F32)],
        compiler_params=LIMIT,
        cost_estimate=cost(27 * LANES),
    )(conv_late, volume, error, slope_early)


def early_grad(core, error_early, volume_t, late, late_other):
    return pl.pallas_call(
        early_grad_kernel,
        out_shape=(EARLY_ROWS, EARLY_ROWS, LATE_ROWS),
        in_specs=[SMEM] + [VMEM] * 4,
        out_specs=(VMEM,) * 3,
        scratch_shapes=[pltpu.VMEM((2, HALF, LANES), BF16)],
        compiler_params=LIMIT,
        cost_estimate=cost(16 * 256),
    )(core, error_early, volume_t, late, late_other)


def ring_place(core):
    return jnp.where(core == 0, lax.axis_index("z"), lax.axis_index("y"))


def chip_routes():
    shifts = [[], [], [], []]
    planes = {}
    for xl in range(2):
        for z in range(RING):
            for core in range(2):
                for y in range(RING):
                    for xh in range(2):
                        index = lambda z, y: (((xl * RING + z) * 2 + core) * RING + y) * 2 + xh
                        for by, pairs in enumerate(shifts):
                            to = ((z + by) % RING, y) if core == 0 else (z, (y + by) % RING)
                            pairs.append((index(z, y), index(*to)))
                        planes.setdefault((core, z if core == 0 else y), []).append(index(z, y))
    return shifts, [planes[key] for key in sorted(planes)]


def small_call(kernel, out_shape, scratch, *args):
    return pl.pallas_call(
        kernel,
        out_shape=out_shape,
        in_specs=[SMEM if arg.ndim == 1 else VMEM for arg in args],
        out_specs=jax.tree.map(lambda _: VMEM, out_shape),
        scratch_shapes=scratch,
        compiler_params=SMALL,
        cost_estimate=pl.CostEstimate(flops=0, bytes_accessed=2 * 1024 * 1024, transcendentals=0),
    )(*args)


def pair_kernel(place, early, early_other, late_sum, *blocks):
    for n, block in enumerate(blocks):
        quarter = (place[0] + n) % RING
        part = pl.ds(pl.multiple_of(quarter * QUARTER, QUARTER), QUARTER)
        block[:QUARTER] = (early[part].astype(F32) + early_other[part].astype(F32)).astype(BF16)
        block[QUARTER:] = late_sum[pl.ds(pl.multiple_of(quarter * QUARTER_LATE, 16), QUARTER_LATE)]


def pair_sums(place, early, early_other, late_sum):
    block = jax.ShapeDtypeStruct((QUARTER + QUARTER_LATE, LANES), BF16)
    return small_call(pair_kernel, (block,) * RING, [], place.reshape(1), early, early_other, late_sum)


def ring_kernel(first, second, third, fourth, shares, late):
    total = first[...].astype(F32) + second[...].astype(F32)
    total = total + third[...].astype(F32) + fourth[...].astype(F32)
    shares[:, :SHARE] = total[:QUARTER].astype(BF16).reshape(16, SHARE, LANES)
    late[:QUARTER_LATE] = total[QUARTER:]
    late[QUARTER_LATE:] = jnp.zeros((late.shape[0] - QUARTER_LATE, LANES), F32)
    for n in range(16):
        shares[n, SHARE:] = late[n * SHARE_LATE : n * SHARE_LATE + SHARE].astype(BF16)


def share_kernel(shares, spread):
    total = jnp.sum(shares[...].astype(F32), axis=0).astype(BF16)
    for n in range(16):
        spread[n] = total


def join_kernel(shares, rows, late):
    rows[:QUARTER] = shares[:, :SHARE].reshape(QUARTER, LANES)
    for n in range(16):
        late[n * SHARE_LATE : n * SHARE_LATE + SHARE] = shares[n, SHARE:].astype(F32)
    rows[QUARTER:] = late[:QUARTER_LATE].astype(BF16)


def swapped(block):
    return lax.ppermute(block, "core", [(0, 1), (1, 0)])


def summed(core, early, early_other, late_sum):
    shifts, planes = chip_routes()
    exchange = lambda blocks: lax.all_to_all(
        blocks, FINE, split_axis=0, concat_axis=0, axis_index_groups=planes, tiled=True
    )
    blocks = list(pair_sums(ring_place(core), early, early_other, late_sum))
    order = (2, 1, 3)
    others = [lax.ppermute(blocks[by], FINE, shifts[by]) for by in order]
    shares = jax.ShapeDtypeStruct((16, 2 * SHARE, LANES), BF16)
    uneven = [pltpu.VMEM((QUARTER_LATE + 8, LANES), F32)]
    sent = exchange(small_call(ring_kernel, shares, uneven, blocks[0], *others))
    spread = exchange(small_call(share_kernel, shares, [], sent))
    rows = jax.ShapeDtypeStruct((QUARTER + QUARTER_LATE, LANES), BF16)
    quarter = small_call(join_kernel, rows, uneven, spread)
    return [quarter] + [lax.ppermute(quarter, FINE, shifts[by]) for by in order]


def place_kernel(origins, where, *refs):
    early, late, wide, sems = refs[-4:]
    copies = []
    for n, (shift, other) in enumerate(origins):
        half = where[0] ^ other
        quarter = (where[1 + other] - shift + RING) % RING
        wide[n] = refs[n][...].astype(F32)
        at_early = pl.multiple_of(half * HALF + quarter * QUARTER, QUARTER)
        at_late = pl.multiple_of(half * HALF_LATE + quarter * QUARTER_LATE, 16)
        copies += [
            pltpu.make_async_copy(
                wide.at[n, pl.ds(0, QUARTER)], early.at[pl.ds(at_early, QUARTER)], sems.at[n, 0]
            ),
            pltpu.make_async_copy(
                wide.at[n, pl.ds(QUARTER, QUARTER_LATE)],
                late.at[pl.ds(at_late, QUARTER_LATE)],
                sems.at[n, 1],
            ),
        ]
        for copy in copies[-2:]:
            copy.start()
    for copy in copies:
        copy.wait()


def placed(where, origins, pieces, so_far):
    count = len(pieces)
    return pl.pallas_call(
        functools.partial(place_kernel, origins),
        out_shape=(
            jax.ShapeDtypeStruct((2 * HALF, LANES), F32),
            jax.ShapeDtypeStruct((2 * HALF_LATE, LANES), F32),
        ),
        in_specs=[SMEM] + [VMEM] * count + [ANY] * len(so_far),
        out_specs=(ANY, ANY),
        input_output_aliases={1 + count + n: n for n in range(len(so_far))},
        scratch_shapes=[
            pltpu.VMEM((count, QUARTER + QUARTER_LATE, LANES), F32),
            pltpu.SemaphoreType.DMA((count, 2)),
        ],
        compiler_params=SMALL,
        cost_estimate=pl.CostEstimate(flops=0, bytes_accessed=count * 768 * 1024, transcendentals=0),
    )(where, *pieces, *so_far)


def per_device(inputs, conv_early, conv_late, cotangent):
    owned = cotangent.shape[0]
    core = lax.axis_index("core")
    sent = inputs.reshape(inputs.shape[0] // owned, owned, inputs.shape[1], SIDE * SIDE, LANES)
    received = lax.all_to_all(sent, ("y", "xh"), split_axis=0, concat_axis=0, tiled=True)
    signal = cotangent.reshape(owned, SIDE * SIDE, SIDE, LANES).swapaxes(0, 1).reshape(CELLS, LANES)
    taps_late = conv_late.reshape(9, 3 * LANES, LANES)
    hidden, volume, slope_early = early_layer(received, conv_early.reshape(16, 2 * LANES, LANES))
    activated, late, late_sent, error = late_layer(core.reshape(1), hidden, taps_late, signal)
    late_other = swapped(late_sent)
    error_early, volume_t = backward(taps_late, volume, error, slope_early)
    early, early_sent, late_sum = early_grad(core.reshape(1), error_early, volume_t, late, late_other)
    zero, two, one, three = summed(core, early, swapped(early_sent), late_sum)
    where = jnp.stack([core, ring_place(core), ring_place(1 - core)])
    totals = placed(where, ((0, 0), (0, 1)), [zero, swapped(zero)], ())
    *totals, three, one, two = lax.optimization_barrier((*totals, three, one, two))
    swaps = [swapped(piece) for piece in (two, one, three)]
    totals = placed(where, ((2, 0), (1, 0)), [two, one], totals)
    early_total, late_total = placed(where, ((3, 0), (2, 1), (1, 1), (3, 1)), [three, *swaps], totals)
    return (
        activated.reshape(cotangent.shape),
        early_total.reshape(conv_early.shape),
        late_total.reshape(conv_late.shape),
    )


def solution(mesh):
    fine = jax.sharding.Mesh(mesh.devices.reshape(2, 4, 2, 4, 2), FINE)
    batch = ("xl", "z", "core")
    every = FINE
    return jax.shard_map(
        per_device,
        mesh=fine,
        in_specs=(
            P(batch, "y", "xh", None, None),
            P(),
            P(),
            P(every, None, None, None, None),
        ),
        out_specs=(P(every, None, None, None, None), P(), P()),
        check_vma=False,
    )
```

```python
import functools

import jax
import jax.numpy as jnp
from jax import lax
from jax.experimental import pallas as pl
from jax.experimental.pallas import tpu as pltpu
from jax.sharding import PartitionSpec as P

FINE = ("xl", "z", "core", "y", "xh")
BF16 = jnp.bfloat16
F32 = jnp.float32
SIDE = 8
LANES = 128
CELLS = SIDE * SIDE * 16
HALF = 4 * 4 * 4 * 64 // 2
HALF_LATE = 3 * 3 * 3 * 128 // 2
GRANULE = HALF_LATE // 9
SHARE = HALF // 64
SHARE_LATE = HALF_LATE // 64
RING = 4
QUARTER = HALF // RING
QUARTER_LATE = HALF_LATE // RING


def shifted(rows, by, lane=None):
    moved = pltpu.roll(rows, by % SIDE, 1)
    width = lax.broadcasted_iota(jnp.int32, rows.shape, 1)
    return jnp.where(width == (0 if by == 1 else SIDE - 1), 0.0, moved)


def three_widths(rows):
    return jnp.concatenate([shifted(rows, 1), rows, shifted(rows, -1)], axis=-1)


def clear_rim(ref, size):
    lanes = ref.shape[-1]
    slab = jnp.zeros((size, 16, lanes), BF16)
    ref[0] = slab
    ref[size - 1] = slab
    ref[:, 0] = slab
    ref[:, size - 1] = slab


def cube_conv(field, blocks, total):
    def product(first, count, weights, transposed):
        rows = jnp.concatenate([field[first : first + count, kh : kh + SIDE] for kh in range(3)], axis=-1)
        dims = (((1,), (1 if transposed else 0,)), ((), ()))
        return lax.dot_general(
            rows.reshape(count * LANES, 9 * LANES), weights, dims, preferred_element_type=F32
        )

    (first, transposed), (second, _), (third, _) = (blocks(kd) for kd in range(3))
    two = product(0, 9, jnp.concatenate([first, second], axis=0 if transposed else 1), transposed)
    total[...] = two[0:CELLS, 0:LANES] + two[LANES : LANES + CELLS, LANES:]
    total[...] += product(2, SIDE, third, transposed)


def early_kernel(received, conv_early, hidden, volume, slope_early, total):
    depth_blocks, height_blocks = 4, 2
    blank = jnp.zeros((9, 16, 2 * LANES), BF16)
    for dp in range(2):
        for hp in range(2):
            volume[2 * dp + hp, 0 if dp else 8] = blank
            volume[2 * dp + hp, :, 0 if hp else 8] = blank

    for block in range(depth_blocks * height_blocks):
        db, hb = divmod(block, height_blocks)
        for layer in range(4):
            half, dp = layer // 2, layer % 2
            samples = [
                received[block, s, layer].astype(F32).reshape(4, 2, SIDE, LANES) for s in range(2)
            ]
            for hp in range(2):
                centre = jnp.stack([x[:, hp] for x in samples], axis=1).reshape(8, SIDE, LANES)
                lane = lax.broadcasted_iota(jnp.int32, centre.shape, 2)
                sides = jnp.where(lane < LANES // 2, shifted(centre, -1), shifted(centre, 1))
                both = jnp.concatenate([centre, sides], axis=-1).reshape(4, 16, 2 * LANES)
                volume[2 * dp + hp, 2 * db + half + dp, 4 * hb + hp : 4 * hb + hp + 4] = both.astype(
                    BF16
                )

    def early_taps(kd, kh):
        tap = 4 * kd + kh
        return jnp.concatenate([conv_early[tap, 64:256], conv_early[tap, 0:64]], axis=0)

    for dp in range(2):
        rows = jnp.concatenate(
            [volume[2 * dp + (kh + 1) % 2, :, kh // 2 : kh // 2 + SIDE] for kh in range(4)], axis=-1
        )
        weights = [
            jnp.concatenate([early_taps(kd, kh) for kh in range(4)], axis=0) for kd in (1 - dp, 3 - dp)
        ]
        two = jnp.dot(
            rows.reshape(9 * LANES, 8 * LANES),
            jnp.concatenate(weights, axis=1),
            preferred_element_type=F32,
        )
        both = two[0:CELLS, 0:LANES] + two[LANES : LANES + CELLS, LANES:]
        if dp:
            total[...] += both
        else:
            total[...] = both

    clear_rim(hidden, 10)
    for d in range(SIDE):
        rows = pl.ds(d * LANES, LANES)
        early = total[rows]
        sigma = jax.nn.sigmoid(early)
        slope_early[rows] = sigma * (1.0 + early * (1.0 - sigma))
        value = (early * sigma).reshape(16, SIDE, LANES)
        hidden[d + 1, 1:9] = three_widths(value).reshape(SIDE, 16, 3 * LANES).astype(BF16)


def late_kernel(
    core, hidden, conv_late, cotangent, activated, kept, sent, error, hidden_t, total, grads
):
    def late_block(kd):
        return conv_late[3 * kd : 3 * kd + 3].reshape(9 * LANES, LANES), False

    cube_conv(hidden, late_block, total)

    clear_rim(error, 10)
    for d in range(SIDE):
        rows = pl.ds(d * LANES, LANES)
        late = total[rows]
        sigma = jax.nn.sigmoid(late)
        out = (late * sigma).reshape(SIDE, 2, SIDE, LANES)
        for s in range(2):
            activated[s, d] = out[:, s].reshape(SIDE * SIDE, LANES).astype(BF16)
        value = (cotangent[rows].astype(F32) * (sigma * (1.0 + late * (1.0 - sigma)))).reshape(16, SIDE, LANES)
        error[d + 1, 1:9] = three_widths(value).reshape(SIDE, 16, 3 * LANES).astype(BF16)

    for d in range(SIDE):
        hidden_t[:, d * LANES : (d + 1) * LANES] = hidden[d + 1, 1:9].reshape(LANES, 3 * LANES).T

    for kh in range(3):
        for depth_taps in ((0, 1), (2,)):
            moved = [
                error[2 - kd : 10 - kd, 2 - kh : 10 - kh, :, LANES : 2 * LANES].reshape(CELLS, LANES)
                for kd in depth_taps
            ]
            side = moved[0] if len(moved) == 1 else jnp.concatenate(moved, axis=1)
            grad = jnp.dot(hidden_t[...], side, preferred_element_type=F32).astype(BF16)
            for column, kd in enumerate(depth_taps):
                for part in range(2):
                    half, granule = divmod(2 * (3 * kd + kh) + part, 9)
                    grads[
                        jnp.where(core[0] == half, 0, 1), granule * GRANULE : (granule + 1) * GRANULE
                    ] = grad[part * GRANULE : (part + 1) * GRANULE, column * LANES : (column + 1) * LANES]
    kept[...] = grads[0]
    sent[...] = grads[1]


def backward_kernel(conv_late, volume, error, slope_early, error_early, volume_t, total):
    clear_rim(error_early, 10)

    def back_block(kd):
        taps = [
            conv_late[3 * (2 - kd) + 2 - kh, (2 - kw) * LANES : (3 - kw) * LANES]
            for kh in range(3)
            for kw in range(3)
        ]
        return jnp.concatenate(taps, axis=1), True

    cube_conv(error, back_block, total)

    for d in range(SIDE):
        rows = pl.ds(d * LANES, LANES)
        value = total[rows].astype(BF16).astype(F32) * slope_early[rows]
        error_early[d + 1, 1:9] = value.astype(BF16).reshape(SIDE, 16, LANES)

    for phase in range(4):
        dp, hp = phase // 2, phase % 2
        for d in range(SIDE):
            volume_t[phase, :, d * LANES : (d + 1) * LANES] = (
                volume[phase, d + dp, hp : hp + SIDE].reshape(LANES, 2 * LANES).T
            )


def early_grad_kernel(core, error_early, volume_t, late, late_other, kept, sent, late_sum, grads):
    late_sum[...] = (late[...].astype(F32) + late_other[...].astype(F32)).astype(BF16)
    for phase in range(4):
        dp, hp = phase // 2, phase % 2
        for first in range(2):
            depth = dp + 1 - first
            moved = [
                error_early[depth : depth + SIDE, hp + 1 - second : hp + 1 - second + SIDE].reshape(
                    CELLS, LANES
                )
                for second in range(2)
            ]
            grad = jnp.dot(
                volume_t[phase], jnp.concatenate(moved, axis=1), preferred_element_type=F32
            ).astype(BF16)
            keep = jnp.where(core[0] == first, 0, 1)
            for second in range(2):
                tap = 4 * (2 * first + 1 - dp) + 2 * second + 1 - hp
                lanes = slice(second * LANES, (second + 1) * LANES)
                at = (tap - 8 * first) * 2 * LANES
                grads[keep, at + 64 : at + 256] = grad[0:192, lanes]
                grads[keep, at : at + 64] = grad[192:256, lanes]
    kept[...] = grads[0]
    sent[...] = grads[1]


VMEM = pl.BlockSpec(memory_space=pltpu.VMEM)
SMEM = pl.BlockSpec(memory_space=pltpu.SMEM)
ANY = pl.BlockSpec(memory_space=pl.ANY)
SMALL = pltpu.CompilerParams(vmem_limit_bytes=12 * 1024 * 1024)
LIMIT = pltpu.CompilerParams(vmem_limit_bytes=24 * 1024 * 1024)
VOLUME = (4, 9, 9, 16, 2 * LANES)
FIELD = (10, 10, 16, 3 * LANES)


EARLY_ROWS = jax.ShapeDtypeStruct((HALF, LANES), BF16)
LATE_ROWS = jax.ShapeDtypeStruct((HALF_LATE, LANES), BF16)


def cost(products, transcendentals=0):
    return pl.CostEstimate(
        flops=2 * CELLS * LANES * products,
        bytes_accessed=8 * 1024 * 1024,
        transcendentals=transcendentals,
    )


def early_layer(received, conv_early):
    return pl.pallas_call(
        early_kernel,
        out_shape=(
            jax.ShapeDtypeStruct(FIELD, BF16),
            jax.ShapeDtypeStruct(VOLUME, BF16),
            jax.ShapeDtypeStruct((CELLS, LANES), F32),
        ),
        in_specs=[VMEM, VMEM],
        out_specs=(VMEM,) * 3,
        scratch_shapes=[pltpu.VMEM((CELLS, LANES), F32)],
        compiler_params=LIMIT,
        cost_estimate=cost(16 * 256, CELLS * LANES),
    )(received, conv_early)


def late_layer(core, hidden, conv_late, cotangent):
    return pl.pallas_call(
        late_kernel,
        out_shape=(
            jax.ShapeDtypeStruct((2, SIDE, SIDE * SIDE, LANES), BF16),
            LATE_ROWS,
            LATE_ROWS,
            jax.ShapeDtypeStruct(FIELD, BF16),
        ),
        in_specs=[SMEM, VMEM, VMEM, VMEM],
        out_specs=(VMEM,) * 4,
        scratch_shapes=[
            pltpu.VMEM((3 * LANES, CELLS), BF16),
            pltpu.VMEM((CELLS, LANES), F32),
            pltpu.VMEM((2, HALF_LATE, LANES), BF16),
        ],
        compiler_params=LIMIT,
        cost_estimate=cost(2 * 27 * LANES, CELLS * LANES),
    )(core, hidden, conv_late, cotangent)


def backward(conv_late, volume, error, slope_early):
    return pl.pallas_call(
        backward_kernel,
        out_shape=(
            jax.ShapeDtypeStruct((10, 10, 16, LANES), BF16),
            jax.ShapeDtypeStruct((4, 2 * LANES, CELLS), BF16),
        ),
        in_specs=[VMEM] * 4,
        out_specs=(VMEM, VMEM),
        scratch_shapes=[pltpu.VMEM((CELLS, LANES), F32)],
        compiler_params=LIMIT,
        cost_estimate=cost(27 * LANES),
    )(conv_late, volume, error, slope_early)


def early_grad(core, error_early, volume_t, late, late_other):
    return pl.pallas_call(
        early_grad_kernel,
        out_shape=(EARLY_ROWS, EARLY_ROWS, LATE_ROWS),
        in_specs=[SMEM] + [VMEM] * 4,
        out_specs=(VMEM,) * 3,
        scratch_shapes=[pltpu.VMEM((2, HALF, LANES), BF16)],
        compiler_params=LIMIT,
        cost_estimate=cost(16 * 256),
    )(core, error_early, volume_t, late, late_other)


def ring_place(core):
    return jnp.where(core == 0, lax.axis_index("z"), lax.axis_index("y"))


def chip_routes():
    shifts = [[], [], [], []]
    planes = {}
    for xl in range(2):
        for z in range(RING):
            for core in range(2):
                for y in range(RING):
                    for xh in range(2):
                        index = lambda z, y: (((xl * RING + z) * 2 + core) * RING + y) * 2 + xh
                        for by, pairs in enumerate(shifts):
                            to = ((z + by) % RING, y) if core == 0 else (z, (y + by) % RING)
                            pairs.append((index(z, y), index(*to)))
                        planes.setdefault((core, z if core == 0 else y), []).append(index(z, y))
    return shifts, [planes[key] for key in sorted(planes)]


def small_call(kernel, out_shape, scratch, *args):
    return pl.pallas_call(
        kernel,
        out_shape=out_shape,
        in_specs=[SMEM if arg.ndim == 1 else VMEM for arg in args],
        out_specs=jax.tree.map(lambda _: VMEM, out_shape),
        scratch_shapes=scratch,
        compiler_params=SMALL,
        cost_estimate=pl.CostEstimate(flops=0, bytes_accessed=2 * 1024 * 1024, transcendentals=0),
    )(*args)


def pair_kernel(place, early, early_other, late_sum, *blocks):
    for n, block in enumerate(blocks):
        quarter = (place[0] + n) % RING
        part = pl.ds(pl.multiple_of(quarter * QUARTER, QUARTER), QUARTER)
        block[:QUARTER] = (early[part].astype(F32) + early_other[part].astype(F32)).astype(BF16)
        block[QUARTER:] = late_sum[pl.ds(pl.multiple_of(quarter * QUARTER_LATE, 16), QUARTER_LATE)]


def pair_sums(place, early, early_other, late_sum):
    block = jax.ShapeDtypeStruct((QUARTER + QUARTER_LATE, LANES), BF16)
    return small_call(pair_kernel, (block,) * RING, [], place.reshape(1), early, early_other, late_sum)


def ring_kernel(first, second, third, fourth, shares, late):
    total = first[...].astype(F32) + second[...].astype(F32)
    total = total + third[...].astype(F32) + fourth[...].astype(F32)
    shares[:, :SHARE] = total[:QUARTER].astype(BF16).reshape(16, SHARE, LANES)
    late[:QUARTER_LATE] = total[QUARTER:]
    late[QUARTER_LATE:] = jnp.zeros((late.shape[0] - QUARTER_LATE, LANES), F32)
    for n in range(16):
        shares[n, SHARE:] = late[n * SHARE_LATE : n * SHARE_LATE + SHARE].astype(BF16)


def share_kernel(shares, spread):
    total = jnp.sum(shares[...].astype(F32), axis=0).astype(BF16)
    for n in range(16):
        spread[n] = total


def join_kernel(shares, rows, late):
    rows[:QUARTER] = shares[:, :SHARE].reshape(QUARTER, LANES)
    for n in range(16):
        late[n * SHARE_LATE : n * SHARE_LATE + SHARE] = shares[n, SHARE:].astype(F32)
    rows[QUARTER:] = late[:QUARTER_LATE].astype(BF16)


def swapped(block):
    return lax.ppermute(block, "core", [(0, 1), (1, 0)])


def summed(core, early, early_other, late_sum):
    shifts, planes = chip_routes()
    exchange = lambda blocks: lax.all_to_all(
        blocks, FINE, split_axis=0, concat_axis=0, axis_index_groups=planes, tiled=True
    )
    blocks = list(pair_sums(ring_place(core), early, early_other, late_sum))
    order = (2, 1, 3)
    others = [lax.ppermute(blocks[by], FINE, shifts[by]) for by in order]
    shares = jax.ShapeDtypeStruct((16, 2 * SHARE, LANES), BF16)
    uneven = [pltpu.VMEM((QUARTER_LATE + 8, LANES), F32)]
    sent = exchange(small_call(ring_kernel, shares, uneven, blocks[0], *others))
    spread = exchange(small_call(share_kernel, shares, [], sent))
    rows = jax.ShapeDtypeStruct((QUARTER + QUARTER_LATE, LANES), BF16)
    quarter = small_call(join_kernel, rows, uneven, spread)
    return [quarter] + [lax.ppermute(quarter, FINE, shifts[by]) for by in order]


def place_kernel(origins, core, place, other_place, *refs):
    early, late, wide, sems = refs[-4:]
    copies = []
    for n, (shift, other) in enumerate(origins):
        half = core[0] ^ other
        quarter = ((other_place if other else place)[0] - shift + RING) % RING
        wide[n] = refs[n][...].astype(F32)
        at_early = pl.multiple_of(half * HALF + quarter * QUARTER, QUARTER)
        at_late = pl.multiple_of(half * HALF_LATE + quarter * QUARTER_LATE, 16)
        copies += [
            pltpu.make_async_copy(
                wide.at[n, pl.ds(0, QUARTER)], early.at[pl.ds(at_early, QUARTER)], sems.at[n, 0]
            ),
            pltpu.make_async_copy(
                wide.at[n, pl.ds(QUARTER, QUARTER_LATE)],
                late.at[pl.ds(at_late, QUARTER_LATE)],
                sems.at[n, 1],
            ),
        ]
        for copy in copies[-2:]:
            copy.start()
    for copy in copies:
        copy.wait()


def placed(scalars, origins, pieces, so_far):
    count = len(pieces)
    return pl.pallas_call(
        functools.partial(place_kernel, origins),
        out_shape=(
            jax.ShapeDtypeStruct((2 * HALF, LANES), F32),
            jax.ShapeDtypeStruct((2 * HALF_LATE, LANES), F32),
        ),
        in_specs=[SMEM] * 3 + [VMEM] * count + [ANY] * len(so_far),
        out_specs=(ANY, ANY),
        input_output_aliases={3 + count + n: n for n in range(len(so_far))},
        scratch_shapes=[
            pltpu.VMEM((count, QUARTER + QUARTER_LATE, LANES), F32),
            pltpu.SemaphoreType.DMA((count, 2)),
        ],
        compiler_params=SMALL,
        cost_estimate=pl.CostEstimate(flops=0, bytes_accessed=count * 768 * 1024, transcendentals=0),
    )(*scalars, *pieces, *so_far)


def per_device(inputs, conv_early, conv_late, cotangent):
    owned = cotangent.shape[0]
    core = lax.axis_index("core")
    sent = inputs.reshape(inputs.shape[0] // owned, owned, inputs.shape[1], SIDE * SIDE, LANES)
    received = lax.all_to_all(sent, ("y", "xh"), split_axis=0, concat_axis=0, tiled=True)
    signal = cotangent.reshape(owned, SIDE * SIDE, SIDE, LANES).swapaxes(0, 1).reshape(CELLS, LANES)
    taps_late = conv_late.reshape(9, 3 * LANES, LANES)
    hidden, volume, slope_early = early_layer(received, conv_early.reshape(16, 2 * LANES, LANES))
    activated, late, late_sent, error = late_layer(core.reshape(1), hidden, taps_late, signal)
    late_other = swapped(late_sent)
    error_early, volume_t = backward(taps_late, volume, error, slope_early)
    early, early_sent, late_sum = early_grad(core.reshape(1), error_early, volume_t, late, late_other)
    zero, two, one, three = summed(core, early, swapped(early_sent), late_sum)
    scalars = [value.reshape(1) for value in (core, ring_place(core), ring_place(1 - core))]
    totals = placed(scalars, ((0, 0), (0, 1)), [zero, swapped(zero)], ())
    *totals, three, one, two = lax.optimization_barrier((*totals, three, one, two))
    swaps = [swapped(piece) for piece in (two, one, three)]
    totals = placed(scalars, ((2, 0), (1, 0)), [two, one], totals)
    early_total, late_total = placed(scalars, ((3, 0), (2, 1), (1, 1), (3, 1)), [three, *swaps], totals)
    return (
        activated.reshape(cotangent.shape),
        early_total.reshape(conv_early.shape),
        late_total.reshape(conv_late.shape),
    )


def solution(mesh):
    fine = jax.sharding.Mesh(mesh.devices.reshape(2, 4, 2, 4, 2), FINE)
    batch = ("xl", "z", "core")
    every = FINE
    return jax.shard_map(
        per_device,
        mesh=fine,
        in_specs=(
            P(batch, "y", "xh", None, None),
            P(),
            P(),
            P(every, None, None, None, None),
        ),
        out_specs=(P(every, None, None, None, None), P(), P()),
        check_vma=False,
    )
```

```python
import functools

import jax
import jax.numpy as jnp
from jax import lax
from jax.experimental import pallas as pl
from jax.experimental.pallas import tpu as pltpu
from jax.sharding import PartitionSpec as P

FINE = ("xl", "z", "core", "y", "xh")
BF16 = jnp.bfloat16
F32 = jnp.float32
SIDE = 8
LANES = 128
CELLS = SIDE * SIDE * 16
HALF = 4 * 4 * 4 * 64 // 2
HALF_LATE = 3 * 3 * 3 * 128 // 2
GRANULE = HALF_LATE // 9
SHARE = HALF // 64
SHARE_LATE = HALF_LATE // 64
RING = 4
QUARTER = HALF // RING
QUARTER_LATE = HALF_LATE // RING


def shifted(rows, by, lane=None):
    moved = pltpu.roll(rows, by % SIDE, 1)
    width = lax.broadcasted_iota(jnp.int32, rows.shape, 1)
    return jnp.where(width == (0 if by == 1 else SIDE - 1), 0.0, moved)


def three_widths(rows):
    return jnp.concatenate([shifted(rows, 1), rows, shifted(rows, -1)], axis=-1)


def clear_rim(ref, size):
    lanes = ref.shape[-1]
    slab = jnp.zeros((size, 16, lanes), BF16)
    ref[0] = slab
    ref[size - 1] = slab
    ref[:, 0] = slab
    ref[:, size - 1] = slab


def cube_conv(field, blocks, total):
    def product(first, count, weights, transposed):
        rows = jnp.concatenate([field[first : first + count, kh : kh + SIDE] for kh in range(3)], axis=-1)
        dims = (((1,), (1 if transposed else 0,)), ((), ()))
        return lax.dot_general(
            rows.reshape(count * LANES, 9 * LANES), weights, dims, preferred_element_type=F32
        )

    (first, transposed), (second, _), (third, _) = (blocks(kd) for kd in range(3))
    two = product(0, 9, jnp.concatenate([first, second], axis=0 if transposed else 1), transposed)
    total[...] = two[0:CELLS, 0:LANES] + two[LANES : LANES + CELLS, LANES:]
    total[...] += product(2, SIDE, third, transposed)


def early_kernel(received, conv_early, hidden, volume, slope_early, total):
    depth_blocks, height_blocks = 4, 2
    blank = jnp.zeros((9, 16, 2 * LANES), BF16)
    for dp in range(2):
        for hp in range(2):
            volume[2 * dp + hp, 0 if dp else 8] = blank
            volume[2 * dp + hp, :, 0 if hp else 8] = blank

    for block in range(depth_blocks * height_blocks):
        db, hb = divmod(block, height_blocks)
        for layer in range(4):
            half, dp = layer // 2, layer % 2
            samples = [
                received[block, s, layer].astype(F32).reshape(4, 2, SIDE, LANES) for s in range(2)
            ]
            for hp in range(2):
                centre = jnp.stack([x[:, hp] for x in samples], axis=1).reshape(8, SIDE, LANES)
                lane = lax.broadcasted_iota(jnp.int32, centre.shape, 2)
                sides = jnp.where(lane < LANES // 2, shifted(centre, -1), shifted(centre, 1))
                both = jnp.concatenate([centre, sides], axis=-1).reshape(4, 16, 2 * LANES)
                volume[2 * dp + hp, 2 * db + half + dp, 4 * hb + hp : 4 * hb + hp + 4] = both.astype(
                    BF16
                )

    def early_taps(kd, kh):
        tap = 4 * kd + kh
        return jnp.concatenate([conv_early[tap, 64:256], conv_early[tap, 0:64]], axis=0)

    for dp in range(2):
        rows = jnp.concatenate(
            [volume[2 * dp + (kh + 1) % 2, :, kh // 2 : kh // 2 + SIDE] for kh in range(4)], axis=-1
        )
        weights = [
            jnp.concatenate([early_taps(kd, kh) for kh in range(4)], axis=0) for kd in (1 - dp, 3 - dp)
        ]
        two = jnp.dot(
            rows.reshape(9 * LANES, 8 * LANES),
            jnp.concatenate(weights, axis=1),
            preferred_element_type=F32,
        )
        both = two[0:CELLS, 0:LANES] + two[LANES : LANES + CELLS, LANES:]
        if dp:
            total[...] += both
        else:
            total[...] = both

    clear_rim(hidden, 10)
    for d in range(SIDE):
        rows = pl.ds(d * LANES, LANES)
        early = total[rows]
        sigma = jax.nn.sigmoid(early)
        slope_early[rows] = sigma * (1.0 + early * (1.0 - sigma))
        value = (early * sigma).reshape(16, SIDE, LANES)
        hidden[d + 1, 1:9] = three_widths(value).reshape(SIDE, 16, 3 * LANES).astype(BF16)


def late_kernel(
    core, hidden, conv_late, cotangent, activated, kept, sent, error, hidden_t, total, grads
):
    def late_block(kd):
        return conv_late[3 * kd : 3 * kd + 3].reshape(9 * LANES, LANES), False

    cube_conv(hidden, late_block, total)

    clear_rim(error, 10)
    for d in range(SIDE):
        rows = pl.ds(d * LANES, LANES)
        late = total[rows]
        sigma = jax.nn.sigmoid(late)
        out = (late * sigma).reshape(SIDE, 2, SIDE, LANES)
        for s in range(2):
            activated[s, d] = out[:, s].reshape(SIDE * SIDE, LANES).astype(BF16)
        value = (cotangent[rows].astype(F32) * (sigma * (1.0 + late * (1.0 - sigma)))).reshape(16, SIDE, LANES)
        error[d + 1, 1:9] = three_widths(value).reshape(SIDE, 16, 3 * LANES).astype(BF16)

    for d in range(SIDE):
        hidden_t[:, d * LANES : (d + 1) * LANES] = hidden[d + 1, 1:9].reshape(LANES, 3 * LANES).T

    for kh in range(3):
        for depth_taps in ((0, 1), (2,)):
            moved = [
                error[2 - kd : 10 - kd, 2 - kh : 10 - kh, :, LANES : 2 * LANES].reshape(CELLS, LANES)
                for kd in depth_taps
            ]
            side = moved[0] if len(moved) == 1 else jnp.concatenate(moved, axis=1)
            grad = jnp.dot(hidden_t[...], side, preferred_element_type=F32).astype(BF16)
            for column, kd in enumerate(depth_taps):
                for part in range(2):
                    half, granule = divmod(2 * (3 * kd + kh) + part, 9)
                    grads[
                        jnp.where(core[0] == half, 0, 1), granule * GRANULE : (granule + 1) * GRANULE
                    ] = grad[part * GRANULE : (part + 1) * GRANULE, column * LANES : (column + 1) * LANES]
    kept[...] = grads[0]
    sent[...] = grads[1]


def backward_kernel(conv_late, volume, error, slope_early, error_early, volume_t, total):
    clear_rim(error_early, 10)

    def back_block(kd):
        taps = [
            conv_late[3 * (2 - kd) + 2 - kh, (2 - kw) * LANES : (3 - kw) * LANES]
            for kh in range(3)
            for kw in range(3)
        ]
        return jnp.concatenate(taps, axis=1), True

    cube_conv(error, back_block, total)

    for d in range(SIDE):
        rows = pl.ds(d * LANES, LANES)
        value = total[rows].astype(BF16).astype(F32) * slope_early[rows]
        error_early[d + 1, 1:9] = value.astype(BF16).reshape(SIDE, 16, LANES)

    for phase in range(4):
        dp, hp = phase // 2, phase % 2
        for d in range(SIDE):
            volume_t[phase, :, d * LANES : (d + 1) * LANES] = (
                volume[phase, d + dp, hp : hp + SIDE].reshape(LANES, 2 * LANES).T
            )


def early_grad_kernel(core, error_early, volume_t, late, late_other, kept, sent, late_sum, grads):
    late_sum[...] = (late[...].astype(F32) + late_other[...].astype(F32)).astype(BF16)
    for phase in range(4):
        dp, hp = phase // 2, phase % 2
        for first in range(2):
            depth = dp + 1 - first
            moved = [
                error_early[depth : depth + SIDE, hp + 1 - second : hp + 1 - second + SIDE].reshape(
                    CELLS, LANES
                )
                for second in range(2)
            ]
            grad = jnp.dot(
                volume_t[phase], jnp.concatenate(moved, axis=1), preferred_element_type=F32
            ).astype(BF16)
            keep = jnp.where(core[0] == first, 0, 1)
            for second in range(2):
                tap = 4 * (2 * first + 1 - dp) + 2 * second + 1 - hp
                lanes = slice(second * LANES, (second + 1) * LANES)
                at = (tap - 8 * first) * 2 * LANES
                grads[keep, at + 64 : at + 256] = grad[0:192, lanes]
                grads[keep, at : at + 64] = grad[192:256, lanes]
    kept[...] = grads[0]
    sent[...] = grads[1]


VMEM = pl.BlockSpec(memory_space=pltpu.VMEM)
SMEM = pl.BlockSpec(memory_space=pltpu.SMEM)
ANY = pl.BlockSpec(memory_space=pl.ANY)
SMALL = pltpu.CompilerParams(vmem_limit_bytes=12 * 1024 * 1024)
LIMIT = pltpu.CompilerParams(vmem_limit_bytes=24 * 1024 * 1024)
VOLUME = (4, 9, 9, 16, 2 * LANES)
FIELD = (10, 10, 16, 3 * LANES)


EARLY_ROWS = jax.ShapeDtypeStruct((HALF, LANES), BF16)
LATE_ROWS = jax.ShapeDtypeStruct((HALF_LATE, LANES), BF16)


def cost(products, transcendentals=0):
    return pl.CostEstimate(
        flops=2 * CELLS * LANES * products,
        bytes_accessed=8 * 1024 * 1024,
        transcendentals=transcendentals,
    )


def early_layer(received, conv_early):
    return pl.pallas_call(
        early_kernel,
        out_shape=(
            jax.ShapeDtypeStruct(FIELD, BF16),
            jax.ShapeDtypeStruct(VOLUME, BF16),
            jax.ShapeDtypeStruct((CELLS, LANES), F32),
        ),
        in_specs=[VMEM, VMEM],
        out_specs=(VMEM,) * 3,
        scratch_shapes=[pltpu.VMEM((CELLS, LANES), F32)],
        compiler_params=LIMIT,
        cost_estimate=cost(16 * 256, CELLS * LANES),
    )(received, conv_early)


def late_layer(core, hidden, conv_late, cotangent):
    return pl.pallas_call(
        late_kernel,
        out_shape=(
            jax.ShapeDtypeStruct((2, SIDE, SIDE * SIDE, LANES), BF16),
            LATE_ROWS,
            LATE_ROWS,
            jax.ShapeDtypeStruct(FIELD, BF16),
        ),
        in_specs=[SMEM, VMEM, VMEM, VMEM],
        out_specs=(VMEM,) * 4,
        scratch_shapes=[
            pltpu.VMEM((3 * LANES, CELLS), BF16),
            pltpu.VMEM((CELLS, LANES), F32),
            pltpu.VMEM((2, HALF_LATE, LANES), BF16),
        ],
        compiler_params=LIMIT,
        cost_estimate=cost(2 * 27 * LANES, CELLS * LANES),
    )(core, hidden, conv_late, cotangent)


def backward(conv_late, volume, error, slope_early):
    return pl.pallas_call(
        backward_kernel,
        out_shape=(
            jax.ShapeDtypeStruct((10, 10, 16, LANES), BF16),
            jax.ShapeDtypeStruct((4, 2 * LANES, CELLS), BF16),
        ),
        in_specs=[VMEM] * 4,
        out_specs=(VMEM, VMEM),
        scratch_shapes=[pltpu.VMEM((CELLS, LANES), F32)],
        compiler_params=LIMIT,
        cost_estimate=cost(27 * LANES),
    )(conv_late, volume, error, slope_early)


def early_grad(core, error_early, volume_t, late, late_other):
    return pl.pallas_call(
        early_grad_kernel,
        out_shape=(EARLY_ROWS, EARLY_ROWS, LATE_ROWS),
        in_specs=[SMEM] + [VMEM] * 4,
        out_specs=(VMEM,) * 3,
        scratch_shapes=[pltpu.VMEM((2, HALF, LANES), BF16)],
        compiler_params=LIMIT,
        cost_estimate=cost(16 * 256),
    )(core, error_early, volume_t, late, late_other)


def ring_place(core):
    return jnp.where(core == 0, lax.axis_index("z"), lax.axis_index("y"))


def chip_routes():
    shifts = [[], [], [], []]
    planes = {}
    for xl in range(2):
        for z in range(RING):
            for core in range(2):
                for y in range(RING):
                    for xh in range(2):
                        index = lambda z, y: (((xl * RING + z) * 2 + core) * RING + y) * 2 + xh
                        for by, pairs in enumerate(shifts):
                            to = ((z + by) % RING, y) if core == 0 else (z, (y + by) % RING)
                            pairs.append((index(z, y), index(*to)))
                        planes.setdefault((core, z if core == 0 else y), []).append(index(z, y))
    return shifts, [planes[key] for key in sorted(planes)]


def small_call(kernel, out_shape, scratch, *args):
    return pl.pallas_call(
        kernel,
        out_shape=out_shape,
        in_specs=[SMEM if arg.ndim == 1 else VMEM for arg in args],
        out_specs=jax.tree.map(lambda _: VMEM, out_shape),
        scratch_shapes=scratch,
        compiler_params=SMALL,
        cost_estimate=pl.CostEstimate(flops=0, bytes_accessed=2 * 1024 * 1024, transcendentals=0),
    )(*args)


def pair_kernel(place, early, early_other, late_sum, *blocks):
    for n, block in enumerate(blocks):
        quarter = (place[0] + n) % RING
        part = pl.ds(pl.multiple_of(quarter * QUARTER, QUARTER), QUARTER)
        block[:QUARTER] = (early[part].astype(F32) + early_other[part].astype(F32)).astype(BF16)
        block[QUARTER:] = late_sum[pl.ds(pl.multiple_of(quarter * QUARTER_LATE, 16), QUARTER_LATE)]


def pair_sums(place, early, early_other, late_sum):
    block = jax.ShapeDtypeStruct((QUARTER + QUARTER_LATE, LANES), BF16)
    return small_call(pair_kernel, (block,) * RING, [], place.reshape(1), early, early_other, late_sum)


def ring_kernel(first, second, third, fourth, shares, late):
    total = first[...].astype(F32) + second[...].astype(F32)
    total = total + third[...].astype(F32) + fourth[...].astype(F32)
    shares[:, :SHARE] = total[:QUARTER].astype(BF16).reshape(16, SHARE, LANES)
    late[:QUARTER_LATE] = total[QUARTER:]
    late[QUARTER_LATE:] = jnp.zeros((late.shape[0] - QUARTER_LATE, LANES), F32)
    for n in range(16):
        shares[n, SHARE:] = late[n * SHARE_LATE : n * SHARE_LATE + SHARE].astype(BF16)


def share_kernel(shares, spread):
    total = jnp.sum(shares[...].astype(F32), axis=0).astype(BF16)
    for n in range(16):
        spread[n] = total


def join_kernel(shares, rows, late):
    rows[:QUARTER] = shares[:, :SHARE].reshape(QUARTER, LANES)
    for n in range(16):
        late[n * SHARE_LATE : n * SHARE_LATE + SHARE] = shares[n, SHARE:].astype(F32)
    rows[QUARTER:] = late[:QUARTER_LATE].astype(BF16)


def swapped(block):
    return lax.ppermute(block, "core", [(0, 1), (1, 0)])


def summed(core, early, early_other, late_sum):
    shifts, planes = chip_routes()
    exchange = lambda blocks: lax.all_to_all(
        blocks, FINE, split_axis=0, concat_axis=0, axis_index_groups=planes, tiled=True
    )
    blocks = list(pair_sums(ring_place(core), early, early_other, late_sum))
    order = (2, 1, 3)
    others = [lax.ppermute(blocks[by], FINE, shifts[by]) for by in order]
    shares = jax.ShapeDtypeStruct((16, 2 * SHARE, LANES), BF16)
    uneven = [pltpu.VMEM((QUARTER_LATE + 8, LANES), F32)]
    sent = exchange(small_call(ring_kernel, shares, uneven, blocks[0], *others))
    spread = exchange(small_call(share_kernel, shares, [], sent))
    rows = jax.ShapeDtypeStruct((QUARTER + QUARTER_LATE, LANES), BF16)
    quarter = small_call(join_kernel, rows, uneven, spread)
    return [quarter] + [lax.ppermute(quarter, FINE, shifts[by]) for by in order]


def place_kernel(origins, core, place, other_place, *refs):
    early, late, wide, sems = refs[-4:]
    copies = []
    for n, (shift, other) in enumerate(origins):
        half = core[0] ^ other
        quarter = ((other_place if other else place)[0] - shift + RING) % RING
        wide[n] = refs[n][...].astype(F32)
        at_early = pl.multiple_of(half * HALF + quarter * QUARTER, QUARTER)
        at_late = pl.multiple_of(half * HALF_LATE + quarter * QUARTER_LATE, 16)
        copies += [
            pltpu.make_async_copy(
                wide.at[n, pl.ds(0, QUARTER)], early.at[pl.ds(at_early, QUARTER)], sems.at[n, 0]
            ),
            pltpu.make_async_copy(
                wide.at[n, pl.ds(QUARTER, QUARTER_LATE)],
                late.at[pl.ds(at_late, QUARTER_LATE)],
                sems.at[n, 1],
            ),
        ]
        for copy in copies[-2:]:
            copy.start()
    for copy in copies:
        copy.wait()


def placed(scalars, origins, pieces, so_far):
    count = len(pieces)
    return pl.pallas_call(
        functools.partial(place_kernel, origins),
        out_shape=(
            jax.ShapeDtypeStruct((2 * HALF, LANES), F32),
            jax.ShapeDtypeStruct((2 * HALF_LATE, LANES), F32),
        ),
        in_specs=[SMEM] * 3 + [VMEM] * count + [ANY] * len(so_far),
        out_specs=(ANY, ANY),
        input_output_aliases={3 + count + n: n for n in range(len(so_far))},
        scratch_shapes=[
            pltpu.VMEM((count, QUARTER + QUARTER_LATE, LANES), F32),
            pltpu.SemaphoreType.DMA((count, 2)),
        ],
        compiler_params=SMALL,
        cost_estimate=pl.CostEstimate(flops=0, bytes_accessed=count * 768 * 1024, transcendentals=0),
    )(*scalars, *pieces, *so_far)


def per_device(inputs, conv_early, conv_late, cotangent):
    owned = cotangent.shape[0]
    core = lax.axis_index("core")
    sent = inputs.reshape(inputs.shape[0] // owned, owned, inputs.shape[1], SIDE * SIDE, LANES)
    received = lax.all_to_all(sent, ("y", "xh"), split_axis=0, concat_axis=0, tiled=True)
    signal = cotangent.reshape(owned, SIDE * SIDE, SIDE, LANES).swapaxes(0, 1).reshape(CELLS, LANES)
    taps_late = conv_late.reshape(9, 3 * LANES, LANES)
    hidden, volume, slope_early = early_layer(received, conv_early.reshape(16, 2 * LANES, LANES))
    activated, late, late_sent, error = late_layer(core.reshape(1), hidden, taps_late, signal)
    late_other = swapped(late_sent)
    error_early, volume_t = backward(taps_late, volume, error, slope_early)
    early, early_sent, late_sum = early_grad(core.reshape(1), error_early, volume_t, late, late_other)
    zero, two, one, three = summed(core, early, swapped(early_sent), late_sum)
    scalars = [value.reshape(1) for value in (core, ring_place(core), ring_place(1 - core))]
    totals = placed(scalars, ((0, 0), (0, 1)), [zero, swapped(zero)], ())
    *totals, three, one = lax.optimization_barrier((*totals, three, one))
    totals = placed(scalars, ((2, 0), (2, 1)), [two, swapped(two)], totals)
    early_total, late_total = placed(
        scalars, ((1, 0), (3, 0), (1, 1), (3, 1)), [one, three, swapped(one), swapped(three)], totals
    )
    return (
        activated.reshape(cotangent.shape),
        early_total.reshape(conv_early.shape),
        late_total.reshape(conv_late.shape),
    )


def solution(mesh):
    fine = jax.sharding.Mesh(mesh.devices.reshape(2, 4, 2, 4, 2), FINE)
    batch = ("xl", "z", "core")
    every = FINE
    return jax.shard_map(
        per_device,
        mesh=fine,
        in_specs=(
            P(batch, "y", "xh", None, None),
            P(),
            P(),
            P(every, None, None, None, None),
        ),
        out_specs=(P(every, None, None, None, None), P(), P()),
        check_vma=False,
    )
```

```python
import functools

import jax
import jax.numpy as jnp
from jax import lax
from jax.experimental import pallas as pl
from jax.experimental.pallas import tpu as pltpu
from jax.sharding import PartitionSpec as P

FINE = ("xl", "z", "core", "y", "xh")
BF16 = jnp.bfloat16
F32 = jnp.float32
SIDE = 8
LANES = 128
CELLS = SIDE * SIDE * 16
HALF = 4 * 4 * 4 * 64 // 2
HALF_LATE = 3 * 3 * 3 * 128 // 2
GRANULE = HALF_LATE // 9
SHARE = HALF // 64
SHARE_LATE = HALF_LATE // 64
RING = 4
QUARTER = HALF // RING
QUARTER_LATE = HALF_LATE // RING


def shifted(rows, by, lane=None):
    moved = pltpu.roll(rows, by % SIDE, 1)
    width = lax.broadcasted_iota(jnp.int32, rows.shape, 1)
    return jnp.where(width == (0 if by == 1 else SIDE - 1), 0.0, moved)


def three_widths(rows):
    return jnp.concatenate([shifted(rows, 1), rows, shifted(rows, -1)], axis=-1)


def clear_rim(ref, size):
    lanes = ref.shape[-1]
    slab = jnp.zeros((size, 16, lanes), BF16)
    ref[0] = slab
    ref[size - 1] = slab
    ref[:, 0] = slab
    ref[:, size - 1] = slab


def cube_conv(field, blocks, total):
    def product(first, count, weights, transposed):
        rows = jnp.concatenate([field[first : first + count, kh : kh + SIDE] for kh in range(3)], axis=-1)
        dims = (((1,), (1 if transposed else 0,)), ((), ()))
        return lax.dot_general(
            rows.reshape(count * LANES, 9 * LANES), weights, dims, preferred_element_type=F32
        )

    (first, transposed), (second, _), (third, _) = (blocks(kd) for kd in range(3))
    two = product(0, 9, jnp.concatenate([first, second], axis=0 if transposed else 1), transposed)
    total[...] = two[0:CELLS, 0:LANES] + two[LANES : LANES + CELLS, LANES:]
    total[...] += product(2, SIDE, third, transposed)


def early_kernel(received, conv_early, hidden, volume, slope_early, total):
    depth_blocks, height_blocks = 4, 2
    blank = jnp.zeros((9, 16, 2 * LANES), BF16)
    for dp in range(2):
        for hp in range(2):
            volume[2 * dp + hp, 0 if dp else 8] = blank
            volume[2 * dp + hp, :, 0 if hp else 8] = blank

    for block in range(depth_blocks * height_blocks):
        db, hb = divmod(block, height_blocks)
        for layer in range(4):
            half, dp = layer // 2, layer % 2
            samples = [
                received[block, s, layer].astype(F32).reshape(4, 2, SIDE, LANES) for s in range(2)
            ]
            for hp in range(2):
                centre = jnp.stack([x[:, hp] for x in samples], axis=1).reshape(8, SIDE, LANES)
                lane = lax.broadcasted_iota(jnp.int32, centre.shape, 2)
                sides = jnp.where(lane < LANES // 2, shifted(centre, -1), shifted(centre, 1))
                both = jnp.concatenate([centre, sides], axis=-1).reshape(4, 16, 2 * LANES)
                volume[2 * dp + hp, 2 * db + half + dp, 4 * hb + hp : 4 * hb + hp + 4] = both.astype(
                    BF16
                )

    def early_taps(kd, kh):
        tap = 4 * kd + kh
        return jnp.concatenate([conv_early[tap, 64:256], conv_early[tap, 0:64]], axis=0)

    for dp in range(2):
        rows = jnp.concatenate(
            [volume[2 * dp + (kh + 1) % 2, :, kh // 2 : kh // 2 + SIDE] for kh in range(4)], axis=-1
        )
        weights = [
            jnp.concatenate([early_taps(kd, kh) for kh in range(4)], axis=0) for kd in (1 - dp, 3 - dp)
        ]
        two = jnp.dot(
            rows.reshape(9 * LANES, 8 * LANES),
            jnp.concatenate(weights, axis=1),
            preferred_element_type=F32,
        )
        both = two[0:CELLS, 0:LANES] + two[LANES : LANES + CELLS, LANES:]
        if dp:
            total[...] += both
        else:
            total[...] = both

    clear_rim(hidden, 10)
    for d in range(SIDE):
        rows = pl.ds(d * LANES, LANES)
        early = total[rows]
        sigma = jax.nn.sigmoid(early)
        slope_early[rows] = sigma * (1.0 + early * (1.0 - sigma))
        value = (early * sigma).reshape(16, SIDE, LANES)
        hidden[d + 1, 1:9] = three_widths(value).reshape(SIDE, 16, 3 * LANES).astype(BF16)


def late_kernel(
    core, hidden, conv_late, cotangent, activated, kept, sent, error, hidden_t, total, grads
):
    def late_block(kd):
        return conv_late[3 * kd : 3 * kd + 3].reshape(9 * LANES, LANES), False

    cube_conv(hidden, late_block, total)

    clear_rim(error, 10)
    for d in range(SIDE):
        rows = pl.ds(d * LANES, LANES)
        late = total[rows]
        sigma = jax.nn.sigmoid(late)
        out = (late * sigma).reshape(SIDE, 2, SIDE, LANES)
        for s in range(2):
            activated[s, d] = out[:, s].reshape(SIDE * SIDE, LANES).astype(BF16)
        value = (cotangent[rows].astype(F32) * (sigma * (1.0 + late * (1.0 - sigma)))).reshape(16, SIDE, LANES)
        error[d + 1, 1:9] = three_widths(value).reshape(SIDE, 16, 3 * LANES).astype(BF16)

    for d in range(SIDE):
        hidden_t[:, d * LANES : (d + 1) * LANES] = hidden[d + 1, 1:9].reshape(LANES, 3 * LANES).T

    for kh in range(3):
        for depth_taps in ((0, 1), (2,)):
            moved = [
                error[2 - kd : 10 - kd, 2 - kh : 10 - kh, :, LANES : 2 * LANES].reshape(CELLS, LANES)
                for kd in depth_taps
            ]
            side = moved[0] if len(moved) == 1 else jnp.concatenate(moved, axis=1)
            grad = jnp.dot(hidden_t[...], side, preferred_element_type=F32).astype(BF16)
            for column, kd in enumerate(depth_taps):
                for part in range(2):
                    half, granule = divmod(2 * (3 * kd + kh) + part, 9)
                    grads[
                        jnp.where(core[0] == half, 0, 1), granule * GRANULE : (granule + 1) * GRANULE
                    ] = grad[part * GRANULE : (part + 1) * GRANULE, column * LANES : (column + 1) * LANES]
    kept[...] = grads[0]
    sent[...] = grads[1]


def backward_kernel(conv_late, volume, error, slope_early, error_early, volume_t, total):
    clear_rim(error_early, 10)

    def back_block(kd):
        taps = [
            conv_late[3 * (2 - kd) + 2 - kh, (2 - kw) * LANES : (3 - kw) * LANES]
            for kh in range(3)
            for kw in range(3)
        ]
        return jnp.concatenate(taps, axis=1), True

    cube_conv(error, back_block, total)

    for d in range(SIDE):
        rows = pl.ds(d * LANES, LANES)
        value = total[rows].astype(BF16).astype(F32) * slope_early[rows]
        error_early[d + 1, 1:9] = value.astype(BF16).reshape(SIDE, 16, LANES)

    for phase in range(4):
        dp, hp = phase // 2, phase % 2
        for d in range(SIDE):
            volume_t[phase, :, d * LANES : (d + 1) * LANES] = (
                volume[phase, d + dp, hp : hp + SIDE].reshape(LANES, 2 * LANES).T
            )


def early_grad_kernel(core, error_early, volume_t, late, late_other, kept, sent, late_sum, grads):
    late_sum[...] = (late[...].astype(F32) + late_other[...].astype(F32)).astype(BF16)
    for phase in range(4):
        dp, hp = phase // 2, phase % 2
        for first in range(2):
            depth = dp + 1 - first
            moved = [
                error_early[depth : depth + SIDE, hp + 1 - second : hp + 1 - second + SIDE].reshape(
                    CELLS, LANES
                )
                for second in range(2)
            ]
            grad = jnp.dot(
                volume_t[phase], jnp.concatenate(moved, axis=1), preferred_element_type=F32
            ).astype(BF16)
            keep = jnp.where(core[0] == first, 0, 1)
            for second in range(2):
                tap = 4 * (2 * first + 1 - dp) + 2 * second + 1 - hp
                lanes = slice(second * LANES, (second + 1) * LANES)
                at = (tap - 8 * first) * 2 * LANES
                grads[keep, at + 64 : at + 256] = grad[0:192, lanes]
                grads[keep, at : at + 64] = grad[192:256, lanes]
    kept[...] = grads[0]
    sent[...] = grads[1]


VMEM = pl.BlockSpec(memory_space=pltpu.VMEM)
SMEM = pl.BlockSpec(memory_space=pltpu.SMEM)
ANY = pl.BlockSpec(memory_space=pl.ANY)
SMALL = pltpu.CompilerParams(vmem_limit_bytes=12 * 1024 * 1024)
LIMIT = pltpu.CompilerParams(vmem_limit_bytes=24 * 1024 * 1024)
VOLUME = (4, 9, 9, 16, 2 * LANES)
FIELD = (10, 10, 16, 3 * LANES)


EARLY_ROWS = jax.ShapeDtypeStruct((HALF, LANES), BF16)
LATE_ROWS = jax.ShapeDtypeStruct((HALF_LATE, LANES), BF16)


def cost(products, transcendentals=0):
    return pl.CostEstimate(
        flops=2 * CELLS * LANES * products,
        bytes_accessed=8 * 1024 * 1024,
        transcendentals=transcendentals,
    )


def early_layer(received, conv_early):
    return pl.pallas_call(
        early_kernel,
        out_shape=(
            jax.ShapeDtypeStruct(FIELD, BF16),
            jax.ShapeDtypeStruct(VOLUME, BF16),
            jax.ShapeDtypeStruct((CELLS, LANES), F32),
        ),
        in_specs=[VMEM, VMEM],
        out_specs=(VMEM,) * 3,
        scratch_shapes=[pltpu.VMEM((CELLS, LANES), F32)],
        compiler_params=LIMIT,
        cost_estimate=cost(16 * 256, CELLS * LANES),
    )(received, conv_early)


def late_layer(core, hidden, conv_late, cotangent):
    return pl.pallas_call(
        late_kernel,
        out_shape=(
            jax.ShapeDtypeStruct((2, SIDE, SIDE * SIDE, LANES), BF16),
            LATE_ROWS,
            LATE_ROWS,
            jax.ShapeDtypeStruct(FIELD, BF16),
        ),
        in_specs=[SMEM, VMEM, VMEM, VMEM],
        out_specs=(VMEM,) * 4,
        scratch_shapes=[
            pltpu.VMEM((3 * LANES, CELLS), BF16),
            pltpu.VMEM((CELLS, LANES), F32),
            pltpu.VMEM((2, HALF_LATE, LANES), BF16),
        ],
        compiler_params=LIMIT,
        cost_estimate=cost(2 * 27 * LANES, CELLS * LANES),
    )(core, hidden, conv_late, cotangent)


def backward(conv_late, volume, error, slope_early):
    return pl.pallas_call(
        backward_kernel,
        out_shape=(
            jax.ShapeDtypeStruct((10, 10, 16, LANES), BF16),
            jax.ShapeDtypeStruct((4, 2 * LANES, CELLS), BF16),
        ),
        in_specs=[VMEM] * 4,
        out_specs=(VMEM, VMEM),
        scratch_shapes=[pltpu.VMEM((CELLS, LANES), F32)],
        compiler_params=LIMIT,
        cost_estimate=cost(27 * LANES),
    )(conv_late, volume, error, slope_early)


def early_grad(core, error_early, volume_t, late, late_other):
    return pl.pallas_call(
        early_grad_kernel,
        out_shape=(EARLY_ROWS, EARLY_ROWS, LATE_ROWS),
        in_specs=[SMEM] + [VMEM] * 4,
        out_specs=(VMEM,) * 3,
        scratch_shapes=[pltpu.VMEM((2, HALF, LANES), BF16)],
        compiler_params=LIMIT,
        cost_estimate=cost(16 * 256),
    )(core, error_early, volume_t, late, late_other)


def ring_place(core):
    return jnp.where(core == 0, lax.axis_index("z"), lax.axis_index("y"))


def chip_routes():
    shifts = [[], [], [], []]
    planes = {}
    for xl in range(2):
        for z in range(RING):
            for core in range(2):
                for y in range(RING):
                    for xh in range(2):
                        index = lambda z, y: (((xl * RING + z) * 2 + core) * RING + y) * 2 + xh
                        for by, pairs in enumerate(shifts):
                            to = ((z + by) % RING, y) if core == 0 else (z, (y + by) % RING)
                            pairs.append((index(z, y), index(*to)))
                        planes.setdefault((core, z if core == 0 else y), []).append(index(z, y))
    return shifts, [planes[key] for key in sorted(planes)]


def small_call(kernel, out_shape, scratch, *args):
    return pl.pallas_call(
        kernel,
        out_shape=out_shape,
        in_specs=[SMEM if arg.ndim == 1 else VMEM for arg in args],
        out_specs=jax.tree.map(lambda _: VMEM, out_shape),
        scratch_shapes=scratch,
        compiler_params=SMALL,
        cost_estimate=pl.CostEstimate(flops=0, bytes_accessed=2 * 1024 * 1024, transcendentals=0),
    )(*args)


def pair_kernel(place, early, early_other, late_sum, *blocks):
    for n, block in enumerate(blocks):
        quarter = (place[0] + n) % RING
        part = pl.ds(pl.multiple_of(quarter * QUARTER, QUARTER), QUARTER)
        block[:QUARTER] = (early[part].astype(F32) + early_other[part].astype(F32)).astype(BF16)
        block[QUARTER:] = late_sum[pl.ds(pl.multiple_of(quarter * QUARTER_LATE, 16), QUARTER_LATE)]


def pair_sums(place, early, early_other, late_sum):
    block = jax.ShapeDtypeStruct((QUARTER + QUARTER_LATE, LANES), BF16)
    return small_call(pair_kernel, (block,) * RING, [], place.reshape(1), early, early_other, late_sum)


def ring_kernel(first, second, third, fourth, shares, late):
    total = first[...].astype(F32) + second[...].astype(F32)
    total = total + third[...].astype(F32) + fourth[...].astype(F32)
    shares[:, :SHARE] = total[:QUARTER].astype(BF16).reshape(16, SHARE, LANES)
    late[:QUARTER_LATE] = total[QUARTER:]
    late[QUARTER_LATE:] = jnp.zeros((late.shape[0] - QUARTER_LATE, LANES), F32)
    for n in range(16):
        shares[n, SHARE:] = late[n * SHARE_LATE : n * SHARE_LATE + SHARE].astype(BF16)


def share_kernel(shares, spread):
    total = jnp.sum(shares[...].astype(F32), axis=0).astype(BF16)
    for n in range(16):
        spread[n] = total


def join_kernel(shares, rows, late):
    rows[:QUARTER] = shares[:, :SHARE].reshape(QUARTER, LANES)
    for n in range(16):
        late[n * SHARE_LATE : n * SHARE_LATE + SHARE] = shares[n, SHARE:].astype(F32)
    rows[QUARTER:] = late[:QUARTER_LATE].astype(BF16)


def swapped(block):
    return lax.ppermute(block, "core", [(0, 1), (1, 0)])


def summed(core, early, early_other, late_sum):
    shifts, planes = chip_routes()
    exchange = lambda blocks: lax.all_to_all(
        blocks, FINE, split_axis=0, concat_axis=0, axis_index_groups=planes, tiled=True
    )
    blocks = list(pair_sums(ring_place(core), early, early_other, late_sum))
    order = (2, 1, 3)
    others = [lax.ppermute(blocks[by], FINE, shifts[by]) for by in order]
    shares = jax.ShapeDtypeStruct((16, 2 * SHARE, LANES), BF16)
    uneven = [pltpu.VMEM((QUARTER_LATE + 8, LANES), F32)]
    sent = exchange(small_call(ring_kernel, shares, uneven, blocks[0], *others))
    spread = exchange(small_call(share_kernel, shares, [], sent))
    rows = jax.ShapeDtypeStruct((QUARTER + QUARTER_LATE, LANES), BF16)
    quarter = small_call(join_kernel, rows, uneven, spread)
    return [quarter] + [lax.ppermute(quarter, FINE, shifts[by]) for by in order]


def place_kernel(origins, core, place, other_place, *refs):
    early, late, wide, sems = refs[-4:]
    copies = []
    for n, (shift, other) in enumerate(origins):
        half = core[0] ^ other
        quarter = ((other_place if other else place)[0] - shift + RING) % RING
        wide[n] = refs[n][...].astype(F32)
        at_early = pl.multiple_of(half * HALF + quarter * QUARTER, QUARTER)
        at_late = pl.multiple_of(half * HALF_LATE + quarter * QUARTER_LATE, 16)
        copies += [
            pltpu.make_async_copy(
                wide.at[n, pl.ds(0, QUARTER)], early.at[pl.ds(at_early, QUARTER)], sems.at[n, 0]
            ),
            pltpu.make_async_copy(
                wide.at[n, pl.ds(QUARTER, QUARTER_LATE)],
                late.at[pl.ds(at_late, QUARTER_LATE)],
                sems.at[n, 1],
            ),
        ]
        for copy in copies[-2:]:
            copy.start()
    for copy in copies:
        copy.wait()


def placed(scalars, origins, pieces, so_far):
    count = len(pieces)
    return pl.pallas_call(
        functools.partial(place_kernel, origins),
        out_shape=(
            jax.ShapeDtypeStruct((2 * HALF, LANES), F32),
            jax.ShapeDtypeStruct((2 * HALF_LATE, LANES), F32),
        ),
        in_specs=[SMEM] * 3 + [VMEM] * count + [ANY] * len(so_far),
        out_specs=(ANY, ANY),
        input_output_aliases={3 + count + n: n for n in range(len(so_far))},
        scratch_shapes=[
            pltpu.VMEM((count, QUARTER + QUARTER_LATE, LANES), F32),
            pltpu.SemaphoreType.DMA((count, 2)),
        ],
        compiler_params=SMALL,
        cost_estimate=pl.CostEstimate(flops=0, bytes_accessed=count * 768 * 1024, transcendentals=0),
    )(*scalars, *pieces, *so_far)


def per_device(inputs, conv_early, conv_late, cotangent):
    owned = cotangent.shape[0]
    core = lax.axis_index("core")
    sent = inputs.reshape(inputs.shape[0] // owned, owned, inputs.shape[1], SIDE * SIDE, LANES)
    received = lax.all_to_all(sent, ("y", "xh"), split_axis=0, concat_axis=0, tiled=True)
    signal = cotangent.reshape(owned, SIDE * SIDE, SIDE, LANES).swapaxes(0, 1).reshape(CELLS, LANES)
    taps_late = conv_late.reshape(9, 3 * LANES, LANES)
    hidden, volume, slope_early = early_layer(received, conv_early.reshape(16, 2 * LANES, LANES))
    activated, late, late_sent, error = late_layer(core.reshape(1), hidden, taps_late, signal)
    late_other = swapped(late_sent)
    error_early, volume_t = backward(taps_late, volume, error, slope_early)
    early, early_sent, late_sum = early_grad(core.reshape(1), error_early, volume_t, late, late_other)
    zero, two, one, three = summed(core, early, swapped(early_sent), late_sum)
    scalars = [value.reshape(1) for value in (core, ring_place(core), ring_place(1 - core))]
    totals = placed(scalars, ((0, 0), (0, 1)), [zero, swapped(zero)], ())
    *totals, three, one = lax.optimization_barrier((*totals, three, one))
    swaps = [swapped(one), swapped(three)]
    totals = placed(
        scalars, ((2, 0), (1, 0), (3, 0), (2, 1)), [two, one, three, swapped(two)], totals
    )
    early_total, late_total = placed(scalars, ((1, 1), (3, 1)), swaps, totals)
    return (
        activated.reshape(cotangent.shape),
        early_total.reshape(conv_early.shape),
        late_total.reshape(conv_late.shape),
    )


def solution(mesh):
    fine = jax.sharding.Mesh(mesh.devices.reshape(2, 4, 2, 4, 2), FINE)
    batch = ("xl", "z", "core")
    every = FINE
    return jax.shard_map(
        per_device,
        mesh=fine,
        in_specs=(
            P(batch, "y", "xh", None, None),
            P(),
            P(),
            P(every, None, None, None, None),
        ),
        out_specs=(P(every, None, None, None, None), P(), P()),
        check_vma=False,
    )
```

```python
import functools

import jax
import jax.numpy as jnp
from jax import lax
from jax.experimental import pallas as pl
from jax.experimental.pallas import tpu as pltpu
from jax.sharding import PartitionSpec as P

FINE = ("xl", "z", "core", "y", "xh")
BF16 = jnp.bfloat16
F32 = jnp.float32
SIDE = 8
LANES = 128
CELLS = SIDE * SIDE * 16
HALF = 4 * 4 * 4 * 64 // 2
HALF_LATE = 3 * 3 * 3 * 128 // 2
GRANULE = HALF_LATE // 9
SHARE = HALF // 64
SHARE_LATE = HALF_LATE // 64
RING = 4
QUARTER = HALF // RING
QUARTER_LATE = HALF_LATE // RING


def shifted(rows, by, lane=None):
    moved = pltpu.roll(rows, by % SIDE, 1)
    width = lax.broadcasted_iota(jnp.int32, rows.shape, 1)
    return jnp.where(width == (0 if by == 1 else SIDE - 1), 0.0, moved)


def three_widths(rows):
    return jnp.concatenate([shifted(rows, 1), rows, shifted(rows, -1)], axis=-1)


def clear_rim(ref, size):
    lanes = ref.shape[-1]
    slab = jnp.zeros((size, 16, lanes), BF16)
    ref[0] = slab
    ref[size - 1] = slab
    ref[:, 0] = slab
    ref[:, size - 1] = slab


def cube_conv(field, blocks, total):
    def product(first, count, weights, transposed):
        rows = jnp.concatenate([field[first : first + count, kh : kh + SIDE] for kh in range(3)], axis=-1)
        dims = (((1,), (1 if transposed else 0,)), ((), ()))
        return lax.dot_general(
            rows.reshape(count * LANES, 9 * LANES), weights, dims, preferred_element_type=F32
        )

    (first, transposed), (second, _), (third, _) = (blocks(kd) for kd in range(3))
    two = product(0, 9, jnp.concatenate([first, second], axis=0 if transposed else 1), transposed)
    total[...] = two[0:CELLS, 0:LANES] + two[LANES : LANES + CELLS, LANES:]
    total[...] += product(2, SIDE, third, transposed)


def early_kernel(received, conv_early, hidden, volume, slope_early, total):
    depth_blocks, height_blocks = 4, 2
    blank = jnp.zeros((9, 16, 2 * LANES), BF16)
    for dp in range(2):
        for hp in range(2):
            volume[2 * dp + hp, 0 if dp else 8] = blank
            volume[2 * dp + hp, :, 0 if hp else 8] = blank

    for block in range(depth_blocks * height_blocks):
        db, hb = divmod(block, height_blocks)
        for layer in range(4):
            half, dp = layer // 2, layer % 2
            samples = [
                received[block, s, layer].astype(F32).reshape(4, 2, SIDE, LANES) for s in range(2)
            ]
            for hp in range(2):
                centre = jnp.stack([x[:, hp] for x in samples], axis=1).reshape(8, SIDE, LANES)
                lane = lax.broadcasted_iota(jnp.int32, centre.shape, 2)
                sides = jnp.where(lane < LANES // 2, shifted(centre, -1), shifted(centre, 1))
                both = jnp.concatenate([centre, sides], axis=-1).reshape(4, 16, 2 * LANES)
                volume[2 * dp + hp, 2 * db + half + dp, 4 * hb + hp : 4 * hb + hp + 4] = both.astype(
                    BF16
                )

    def early_taps(kd, kh):
        tap = 4 * kd + kh
        return jnp.concatenate([conv_early[tap, 64:256], conv_early[tap, 0:64]], axis=0)

    for dp in range(2):
        rows = jnp.concatenate(
            [volume[2 * dp + (kh + 1) % 2, :, kh // 2 : kh // 2 + SIDE] for kh in range(4)], axis=-1
        )
        weights = [
            jnp.concatenate([early_taps(kd, kh) for kh in range(4)], axis=0) for kd in (1 - dp, 3 - dp)
        ]
        two = jnp.dot(
            rows.reshape(9 * LANES, 8 * LANES),
            jnp.concatenate(weights, axis=1),
            preferred_element_type=F32,
        )
        both = two[0:CELLS, 0:LANES] + two[LANES : LANES + CELLS, LANES:]
        if dp:
            total[...] += both
        else:
            total[...] = both

    clear_rim(hidden, 10)
    for d in range(SIDE):
        rows = pl.ds(d * LANES, LANES)
        early = total[rows]
        sigma = jax.nn.sigmoid(early)
        slope_early[rows] = sigma * (1.0 + early * (1.0 - sigma))
        value = (early * sigma).reshape(16, SIDE, LANES)
        hidden[d + 1, 1:9] = three_widths(value).reshape(SIDE, 16, 3 * LANES).astype(BF16)


def late_kernel(
    core, hidden, conv_late, cotangent, activated, kept, sent, error, hidden_t, total, grads
):
    def late_block(kd):
        return conv_late[3 * kd : 3 * kd + 3].reshape(9 * LANES, LANES), False

    cube_conv(hidden, late_block, total)

    clear_rim(error, 10)
    for d in range(SIDE):
        rows = pl.ds(d * LANES, LANES)
        late = total[rows]
        sigma = jax.nn.sigmoid(late)
        out = (late * sigma).reshape(SIDE, 2, SIDE, LANES)
        for s in range(2):
            activated[s, d] = out[:, s].reshape(SIDE * SIDE, LANES).astype(BF16)
        value = (cotangent[rows].astype(F32) * (sigma * (1.0 + late * (1.0 - sigma)))).reshape(16, SIDE, LANES)
        error[d + 1, 1:9] = three_widths(value).reshape(SIDE, 16, 3 * LANES).astype(BF16)

    for d in range(SIDE):
        hidden_t[:, d * LANES : (d + 1) * LANES] = hidden[d + 1, 1:9].reshape(LANES, 3 * LANES).T

    for kh in range(3):
        for depth_taps in ((0, 1), (2,)):
            moved = [
                error[2 - kd : 10 - kd, 2 - kh : 10 - kh, :, LANES : 2 * LANES].reshape(CELLS, LANES)
                for kd in depth_taps
            ]
            side = moved[0] if len(moved) == 1 else jnp.concatenate(moved, axis=1)
            grad = jnp.dot(hidden_t[...], side, preferred_element_type=F32).astype(BF16)
            for column, kd in enumerate(depth_taps):
                for part in range(2):
                    half, granule = divmod(2 * (3 * kd + kh) + part, 9)
                    grads[
                        jnp.where(core[0] == half, 0, 1), granule * GRANULE : (granule + 1) * GRANULE
                    ] = grad[part * GRANULE : (part + 1) * GRANULE, column * LANES : (column + 1) * LANES]
    kept[...] = grads[0]
    sent[...] = grads[1]


def backward_kernel(conv_late, volume, error, slope_early, error_early, volume_t, total):
    clear_rim(error_early, 10)

    def back_block(kd):
        taps = [
            conv_late[3 * (2 - kd) + 2 - kh, (2 - kw) * LANES : (3 - kw) * LANES]
            for kh in range(3)
            for kw in range(3)
        ]
        return jnp.concatenate(taps, axis=1), True

    cube_conv(error, back_block, total)

    for d in range(SIDE):
        rows = pl.ds(d * LANES, LANES)
        value = total[rows].astype(BF16).astype(F32) * slope_early[rows]
        error_early[d + 1, 1:9] = value.astype(BF16).reshape(SIDE, 16, LANES)

    for phase in range(4):
        dp, hp = phase // 2, phase % 2
        for d in range(SIDE):
            volume_t[phase, :, d * LANES : (d + 1) * LANES] = (
                volume[phase, d + dp, hp : hp + SIDE].reshape(LANES, 2 * LANES).T
            )


def early_grad_kernel(core, error_early, volume_t, late, late_other, kept, sent, late_sum, grads):
    late_sum[...] = (late[...].astype(F32) + late_other[...].astype(F32)).astype(BF16)
    for phase in range(4):
        dp, hp = phase // 2, phase % 2
        for first in range(2):
            depth = dp + 1 - first
            moved = [
                error_early[depth : depth + SIDE, hp + 1 - second : hp + 1 - second + SIDE].reshape(
                    CELLS, LANES
                )
                for second in range(2)
            ]
            grad = jnp.dot(
                volume_t[phase], jnp.concatenate(moved, axis=1), preferred_element_type=F32
            ).astype(BF16)
            keep = jnp.where(core[0] == first, 0, 1)
            for second in range(2):
                tap = 4 * (2 * first + 1 - dp) + 2 * second + 1 - hp
                lanes = slice(second * LANES, (second + 1) * LANES)
                at = (tap - 8 * first) * 2 * LANES
                grads[keep, at + 64 : at + 256] = grad[0:192, lanes]
                grads[keep, at : at + 64] = grad[192:256, lanes]
    kept[...] = grads[0]
    sent[...] = grads[1]


VMEM = pl.BlockSpec(memory_space=pltpu.VMEM)
SMEM = pl.BlockSpec(memory_space=pltpu.SMEM)
ANY = pl.BlockSpec(memory_space=pl.ANY)
SMALL = pltpu.CompilerParams(vmem_limit_bytes=12 * 1024 * 1024)
LIMIT = pltpu.CompilerParams(vmem_limit_bytes=24 * 1024 * 1024)
VOLUME = (4, 9, 9, 16, 2 * LANES)
FIELD = (10, 10, 16, 3 * LANES)


EARLY_ROWS = jax.ShapeDtypeStruct((HALF, LANES), BF16)
LATE_ROWS = jax.ShapeDtypeStruct((HALF_LATE, LANES), BF16)


def cost(products, transcendentals=0):
    return pl.CostEstimate(
        flops=2 * CELLS * LANES * products,
        bytes_accessed=8 * 1024 * 1024,
        transcendentals=transcendentals,
    )


def early_layer(received, conv_early):
    return pl.pallas_call(
        early_kernel,
        out_shape=(
            jax.ShapeDtypeStruct(FIELD, BF16),
            jax.ShapeDtypeStruct(VOLUME, BF16),
            jax.ShapeDtypeStruct((CELLS, LANES), F32),
        ),
        in_specs=[VMEM, VMEM],
        out_specs=(VMEM,) * 3,
        scratch_shapes=[pltpu.VMEM((CELLS, LANES), F32)],
        compiler_params=LIMIT,
        cost_estimate=cost(16 * 256, CELLS * LANES),
    )(received, conv_early)


def late_layer(core, hidden, conv_late, cotangent):
    return pl.pallas_call(
        late_kernel,
        out_shape=(
            jax.ShapeDtypeStruct((2, SIDE, SIDE * SIDE, LANES), BF16),
            LATE_ROWS,
            LATE_ROWS,
            jax.ShapeDtypeStruct(FIELD, BF16),
        ),
        in_specs=[SMEM, VMEM, VMEM, VMEM],
        out_specs=(VMEM,) * 4,
        scratch_shapes=[
            pltpu.VMEM((3 * LANES, CELLS), BF16),
            pltpu.VMEM((CELLS, LANES), F32),
            pltpu.VMEM((2, HALF_LATE, LANES), BF16),
        ],
        compiler_params=LIMIT,
        cost_estimate=cost(2 * 27 * LANES, CELLS * LANES),
    )(core, hidden, conv_late, cotangent)


def backward(conv_late, volume, error, slope_early):
    return pl.pallas_call(
        backward_kernel,
        out_shape=(
            jax.ShapeDtypeStruct((10, 10, 16, LANES), BF16),
            jax.ShapeDtypeStruct((4, 2 * LANES, CELLS), BF16),
        ),
        in_specs=[VMEM] * 4,
        out_specs=(VMEM, VMEM),
        scratch_shapes=[pltpu.VMEM((CELLS, LANES), F32)],
        compiler_params=LIMIT,
        cost_estimate=cost(27 * LANES),
    )(conv_late, volume, error, slope_early)


def early_grad(core, error_early, volume_t, late, late_other):
    return pl.pallas_call(
        early_grad_kernel,
        out_shape=(EARLY_ROWS, EARLY_ROWS, LATE_ROWS),
        in_specs=[SMEM] + [VMEM] * 4,
        out_specs=(VMEM,) * 3,
        scratch_shapes=[pltpu.VMEM((2, HALF, LANES), BF16)],
        compiler_params=LIMIT,
        cost_estimate=cost(16 * 256),
    )(core, error_early, volume_t, late, late_other)


def ring_place(core):
    return jnp.where(core == 0, lax.axis_index("z"), lax.axis_index("y"))


def chip_routes():
    shifts = [[], [], [], []]
    planes = {}
    for xl in range(2):
        for z in range(RING):
            for core in range(2):
                for y in range(RING):
                    for xh in range(2):
                        index = lambda z, y: (((xl * RING + z) * 2 + core) * RING + y) * 2 + xh
                        for by, pairs in enumerate(shifts):
                            to = ((z + by) % RING, y) if core == 0 else (z, (y + by) % RING)
                            pairs.append((index(z, y), index(*to)))
                        planes.setdefault((core, z if core == 0 else y), []).append(index(z, y))
    return shifts, [planes[key] for key in sorted(planes)]


def small_call(kernel, out_shape, scratch, *args):
    return pl.pallas_call(
        kernel,
        out_shape=out_shape,
        in_specs=[SMEM if arg.ndim == 1 else VMEM for arg in args],
        out_specs=jax.tree.map(lambda _: VMEM, out_shape),
        scratch_shapes=scratch,
        compiler_params=SMALL,
        cost_estimate=pl.CostEstimate(flops=0, bytes_accessed=2 * 1024 * 1024, transcendentals=0),
    )(*args)


def pair_kernel(place, early, early_other, late_sum, *blocks):
    for n, block in enumerate(blocks):
        quarter = (place[0] + n) % RING
        part = pl.ds(pl.multiple_of(quarter * QUARTER, QUARTER), QUARTER)
        block[:QUARTER] = (early[part].astype(F32) + early_other[part].astype(F32)).astype(BF16)
        block[QUARTER:] = late_sum[pl.ds(pl.multiple_of(quarter * QUARTER_LATE, 16), QUARTER_LATE)]


def pair_sums(place, early, early_other, late_sum):
    block = jax.ShapeDtypeStruct((QUARTER + QUARTER_LATE, LANES), BF16)
    return small_call(pair_kernel, (block,) * RING, [], place.reshape(1), early, early_other, late_sum)


def ring_kernel(first, second, third, fourth, shares, late):
    total = first[...].astype(F32) + second[...].astype(F32)
    total = total + third[...].astype(F32) + fourth[...].astype(F32)
    shares[:, :SHARE] = total[:QUARTER].astype(BF16).reshape(16, SHARE, LANES)
    late[:QUARTER_LATE] = total[QUARTER:]
    late[QUARTER_LATE:] = jnp.zeros((late.shape[0] - QUARTER_LATE, LANES), F32)
    for n in range(16):
        shares[n, SHARE:] = late[n * SHARE_LATE : n * SHARE_LATE + SHARE].astype(BF16)


def share_kernel(shares, spread):
    total = jnp.sum(shares[...].astype(F32), axis=0).astype(BF16)
    for n in range(16):
        spread[n] = total


def join_kernel(shares, rows, late):
    rows[:QUARTER] = shares[:, :SHARE].reshape(QUARTER, LANES)
    for n in range(16):
        late[n * SHARE_LATE : n * SHARE_LATE + SHARE] = shares[n, SHARE:].astype(F32)
    rows[QUARTER:] = late[:QUARTER_LATE].astype(BF16)


def swapped(block):
    return lax.ppermute(block, "core", [(0, 1), (1, 0)])


def summed(core, early, early_other, late_sum):
    shifts, planes = chip_routes()
    exchange = lambda blocks: lax.all_to_all(
        blocks, FINE, split_axis=0, concat_axis=0, axis_index_groups=planes, tiled=True
    )
    blocks = list(pair_sums(ring_place(core), early, early_other, late_sum))
    order = (2, 1, 3)
    others = [lax.ppermute(blocks[by], FINE, shifts[by]) for by in order]
    shares = jax.ShapeDtypeStruct((16, 2 * SHARE, LANES), BF16)
    uneven = [pltpu.VMEM((QUARTER_LATE + 8, LANES), F32)]
    sent = exchange(small_call(ring_kernel, shares, uneven, blocks[0], *others))
    spread = exchange(small_call(share_kernel, shares, [], sent))
    rows = jax.ShapeDtypeStruct((QUARTER + QUARTER_LATE, LANES), BF16)
    quarter = small_call(join_kernel, rows, uneven, spread)
    return [quarter] + [lax.ppermute(quarter, FINE, shifts[by]) for by in order]


def place_kernel(origins, core, place, other_place, *refs):
    early, late, wide, sems = refs[-4:]
    copies = []
    for n, (shift, other) in enumerate(origins):
        half = core[0] ^ other
        quarter = ((other_place if other else place)[0] - shift + RING) % RING
        wide[n] = refs[n][...].astype(F32)
        at_early = pl.multiple_of(half * HALF + quarter * QUARTER, QUARTER)
        at_late = pl.multiple_of(half * HALF_LATE + quarter * QUARTER_LATE, 16)
        copies += [
            pltpu.make_async_copy(
                wide.at[n, pl.ds(0, QUARTER)], early.at[pl.ds(at_early, QUARTER)], sems.at[n, 0]
            ),
            pltpu.make_async_copy(
                wide.at[n, pl.ds(QUARTER, QUARTER_LATE)],
                late.at[pl.ds(at_late, QUARTER_LATE)],
                sems.at[n, 1],
            ),
        ]
        for copy in copies[-2:]:
            copy.start()
    for copy in copies:
        copy.wait()


def placed(scalars, origins, pieces, so_far):
    count = len(pieces)
    return pl.pallas_call(
        functools.partial(place_kernel, origins),
        out_shape=(
            jax.ShapeDtypeStruct((2 * HALF, LANES), F32),
            jax.ShapeDtypeStruct((2 * HALF_LATE, LANES), F32),
        ),
        in_specs=[SMEM] * 3 + [VMEM] * count + [ANY] * len(so_far),
        out_specs=(ANY, ANY),
        input_output_aliases={3 + count + n: n for n in range(len(so_far))},
        scratch_shapes=[
            pltpu.VMEM((count, QUARTER + QUARTER_LATE, LANES), F32),
            pltpu.SemaphoreType.DMA((count, 2)),
        ],
        compiler_params=SMALL,
        cost_estimate=pl.CostEstimate(flops=0, bytes_accessed=count * 768 * 1024, transcendentals=0),
    )(*scalars, *pieces, *so_far)


def per_device(inputs, conv_early, conv_late, cotangent):
    owned = cotangent.shape[0]
    core = lax.axis_index("core")
    sent = inputs.reshape(inputs.shape[0] // owned, owned, inputs.shape[1], SIDE * SIDE, LANES)
    received = lax.all_to_all(sent, ("y", "xh"), split_axis=0, concat_axis=0, tiled=True)
    signal = cotangent.reshape(owned, SIDE * SIDE, SIDE, LANES).swapaxes(0, 1).reshape(CELLS, LANES)
    taps_late = conv_late.reshape(9, 3 * LANES, LANES)
    hidden, volume, slope_early = early_layer(received, conv_early.reshape(16, 2 * LANES, LANES))
    activated, late, late_sent, error = late_layer(core.reshape(1), hidden, taps_late, signal)
    late_other = swapped(late_sent)
    error_early, volume_t = backward(taps_late, volume, error, slope_early)
    early, early_sent, late_sum = early_grad(core.reshape(1), error_early, volume_t, late, late_other)
    zero, two, one, three = summed(core, early, swapped(early_sent), late_sum)
    scalars = [value.reshape(1) for value in (core, ring_place(core), ring_place(1 - core))]
    totals = placed(scalars, ((0, 0), (0, 1)), [zero, swapped(zero)], ())
    *totals, three = lax.optimization_barrier((*totals, three))
    swaps = [swapped(one), swapped(three)]
    totals = placed(
        scalars, ((2, 0), (1, 0), (3, 0), (2, 1)), [two, one, three, swapped(two)], totals
    )
    early_total, late_total = placed(scalars, ((1, 1), (3, 1)), swaps, totals)
    return (
        activated.reshape(cotangent.shape),
        early_total.reshape(conv_early.shape),
        late_total.reshape(conv_late.shape),
    )


def solution(mesh):
    fine = jax.sharding.Mesh(mesh.devices.reshape(2, 4, 2, 4, 2), FINE)
    batch = ("xl", "z", "core")
    every = FINE
    return jax.shard_map(
        per_device,
        mesh=fine,
        in_specs=(
            P(batch, "y", "xh", None, None),
            P(),
            P(),
            P(every, None, None, None, None),
        ),
        out_specs=(P(every, None, None, None, None), P(), P()),
        check_vma=False,
    )
```
